512 devices in a mesh: tm: 16 (over z), strip: 32 (over y, x, core).
Axes of the slice: x: 4, y: 4, z: 16, core: 2. Of those that a mesh axis runs over, the one named last changes fastest.
Arguments:
- prev_states: float32 [16, 4, 256, 384], P('tm', None, 'strip'), may hold values from -6 to 6
- observation: bfloat16 [4, 256, 384], P(None, 'strip'), may hold values from -6 to 6
- bounds: int32 [17], replicated, may hold values from 0 to 1000, as said below
- coarse_factor: float32 [16, 4], replicated, may hold values from 0 to 1, as said below
- time_weight: float32 [64], replicated, may hold values from -6 to 6
- weight_in: bfloat16 [3, 3, 64, 8], replicated, may hold values from -1 to 1
- weight_mid: bfloat16 [4, 3, 3, 64, 64], replicated, may hold values from -0.375 to 0.375
- weight_out: bfloat16 [3, 3, 4, 64], replicated, may hold values from -0.375 to 0.375
Outputs:
- new_states: float32 [16, 4, 256, 384], P('tm', None, 'strip')
The draws below stay inside these ranges and needn't reach their ends.
Inputs may be any that keep to these rules, and one draw needn't show every extreme that they name: bounds[0] = 0, bounds[16] = 1000, strictly increasing. `coarse_factor`: every factor lies strictly between 0 and 1.
All inputs are finite; a program needn't handle non-finite values.
Results may differ from the reference program's by a relative error of at most 0.002.
Values may be sent and summed in bfloat16 or wider, within the bound.
No kernel may reach another device: no remote copies, remote signals or barrier semaphores. Data moves between devices by JAX's collectives and lax.ppermute only.
A program may use at most 64 MiB of HBM per device.

```python
import jax
import jax.numpy as jnp
from jax import lax

HIDDEN_FEATURES = 4
HID = 64
LAYERS = 6
STEPS = 1000
COLS = 384
INTERVAL_COUNT = 16
HEIGHT = 256


def draw_bounds(key, part):
    inner = jax.random.permutation(key, STEPS - 1)[:INTERVAL_COUNT - 1] + 1
    inner = jnp.sort(inner.astype(jnp.int32))
    return jnp.concatenate([jnp.zeros((1,), jnp.int32), inner, jnp.full((1,), STEPS, jnp.int32)])


def draw_coarse_factor(key, part):
    selector_seed, speed_seed, jitter_seed, surge_seed, stack_seed = jax.random.split(key, 5)
    slowly = jax.random.permutation(selector_seed, HIDDEN_FEATURES) < HIDDEN_FEATURES // 2
    slow_rate = 0.6 / INTERVAL_COUNT
    fast_rates = jnp.exp(jax.random.uniform(speed_seed, (HIDDEN_FEATURES,), jnp.float32, jnp.log(0.5), jnp.log(1.5)))
    speed_options = jnp.where(slowly, slow_rate, fast_rates)
    jitter_magnitude = jax.random.uniform(jitter_seed, (INTERVAL_COUNT, HIDDEN_FEATURES), jnp.float32, 0.5, 1.5)
    surge_durations = jax.random.uniform(surge_seed, (INTERVAL_COUNT, HIDDEN_FEATURES), jnp.float32) < 2.0 / INTERVAL_COUNT
    stack_heights = jax.random.uniform(stack_seed, (INTERVAL_COUNT, HIDDEN_FEATURES), jnp.float32, 0.6, 0.8)
    return jnp.exp(-speed_options[None, :] * jitter_magnitude) * jnp.where(surge_durations, stack_heights, 1.0)


def steps_of(key, shape, shards, smallest, largest):
    level = 1.0
    for axis_at, shards_of in shards:
        steps = jax.random.uniform(jax.random.fold_in(jax.random.fold_in(key, 6), axis_at), (shards_of,), jnp.float32, smallest / len(shards), largest / len(shards))
        level = level * jnp.repeat(jnp.exp(steps), shape[axis_at] // shards_of).reshape((-1,) + (1,) * (len(shape) - 1 - axis_at))
    return level


def scatter_about(key, extent, scale, reach, cuts=(), kind=jnp.bfloat16):
    values = scale * jax.random.normal(key, extent, jnp.float32)
    if cuts:
        values = values * steps_of(key, extent, cuts, -0.22, 0.18)
    return jnp.clip(values, -reach, reach).astype(kind)


def setup_inputs(seed: int = 0) -> dict:
    key_list = jax.random.split(jax.random.key(seed), 9)
    prev_states = scatter_about(key_list[0], (INTERVAL_COUNT, HIDDEN_FEATURES, HEIGHT, COLS), 1.0, 6.0, ((0, 16), (2, 32)), jnp.float32)
    observation = scatter_about(key_list[1], (HIDDEN_FEATURES, HEIGHT, COLS), 1.0, 6.0, ((1, 32),))
    bounds = draw_bounds(jax.random.fold_in(key_list[8], 71), 0)
    coarse_factor = draw_coarse_factor(jax.random.fold_in(key_list[8], 71), 0)
    time_weight = scatter_about(key_list[4], (HID,), 1.0, 6.0, (), jnp.float32)
    weight_in = scatter_about(key_list[5], (3, 3, HID, 2 * HIDDEN_FEATURES), (9 * HIDDEN_FEATURES) ** -0.5, 1.0)
    weight_mid = scatter_about(key_list[6], (LAYERS - 2, 3, 3, HID, HID), (9 * HID // 2) ** -0.5, 0.375)
    weight_out = scatter_about(key_list[7], (3, 3, HIDDEN_FEATURES, HID), (9 * HID // 2) ** -0.5, 0.375)
    return dict(prev_states=prev_states, observation=observation, bounds=bounds, coarse_factor=coarse_factor, time_weight=time_weight, weight_in=weight_in, weight_mid=weight_mid, weight_out=weight_out)


def convolve(layer_in, weight):
    kernel = jnp.transpose(weight, (2, 3, 0, 1)).astype(jnp.float32)
    summed = lax.conv_general_dilated(layer_in.astype(jnp.float32)[None], kernel, (1, 1), ((1, 1), (1, 1)), dimension_numbers=("NCHW", "OIHW", "NCHW"), precision=lax.Precision.HIGHEST)
    return summed[0]


def velocity_of(state, observation, time_now, time_weight, weight_in, weight_mid, weight_out):
    features = jnp.concatenate([state.astype(jnp.bfloat16), observation], axis=0)
    hidden = jax.nn.silu(convolve(features, weight_in) + time_now * time_weight[:, None, None]).astype(jnp.bfloat16)
    for level in range(LAYERS - 2):
        hidden = jax.nn.silu(convolve(hidden, weight_mid[level])).astype(jnp.bfloat16)
    return convolve(hidden, weight_out)


def reference(prev_states, observation, bounds, coarse_factor, time_weight, weight_in, weight_mid, weight_out):
    def one_slice(packed):
        state, factor, begin, finish, index = packed
        time_now = begin.astype(jnp.float32) / STEPS
        time_step = (finish - begin).astype(jnp.float32) / STEPS
        velocity = velocity_of(state, observation, time_now, time_weight, weight_in, weight_mid, weight_out)
        fine = state + time_step * velocity
        keeper = (index != 0).astype(jnp.float32)
        return fine - keeper * factor[:, None, None] * state

    indices = jnp.arange(INTERVAL_COUNT).astype(jnp.int32)
    jumps = lax.map(one_slice, (prev_states, coarse_factor, bounds[:-1], bounds[1:], indices))

    def advance(carried, packed):
        factor, jump = packed
        result = factor[:, None, None] * carried + jump
        return result, result

    start = jnp.zeros(prev_states.shape[1:], jnp.float32)
    ignored, new_states = lax.scan(advance, start, (coarse_factor, jumps))
    return new_states
```

```python
import jax
import jax.numpy as jnp
from jax import lax
from jax.experimental import pallas as pl
from jax.experimental.pallas import tpu as pltpu
from jax.sharding import PartitionSpec as P

LAYERS = 6
STEPS = 1000
HID = 64
ROWS = 8
COLS = 384
SLABS = 12
LANE_ROWS = 16
PAIRS = SLABS * LANE_ROWS
CHUNK = 2
NT = (((1,), (1,)), ((), ()))


def weights_kernel(mid_ref, first_ref, last_ref, wide_ref, first_out, last_out):
    def pairs_of(taps):
        zero = jnp.zeros_like(taps[0])
        join = lambda a, b: jnp.concatenate([a, b], axis=1)
        return (
            (join(taps[1], taps[2]), join(taps[0], taps[1])),
            (join(zero, taps[0]), join(taps[2], zero)),
        )

    for level in range(LAYERS - 2):
        sets = [pairs_of([mid_ref[level, i, j] * 0.5 for j in range(3)]) for i in range(3)]
        for tile in range(4):
            for r in range(2):
                for c in range(2):
                    for half in range(2):
                        i = 2 * (tile % 2) + half - r
                        block = sets[i][tile // 2][c] if 0 <= i < 3 else jnp.zeros((HID, 2 * HID), jnp.bfloat16)
                        at = (2 * r + c) * HID
                        wide_ref[level, tile, at : at + HID, 128 * half : 128 * half + 128] = block
    sets = [pairs_of([last_ref[i, j] for j in range(3)]) for i in range(3)]
    for tile in range(4):
        for r in range(2):
            for c in range(2):
                for half in range(2):
                    i = 2 * (tile % 2) + half - r
                    block = sets[i][tile // 2][c] if 0 <= i < 3 else jnp.zeros((16, 2 * HID), jnp.bfloat16)
                    at = (2 * c + r) * 16
                    last_out[tile, at : at + 16, 128 * half : 128 * half + 128] = block
    taps = first_ref[...] * 0.5
    lane = lax.broadcasted_iota(jnp.int32, (72, 256), 1)
    place = lax.broadcasted_iota(jnp.int32, (72, 256), 0)
    channel = (lane % 64) // 8
    row = lane % 8
    for order in range(2):
        column = (lane // 64) ^ order
        for step in range(3):
            for r in range(2):
                for c in range(2):
                    i = row - 2 * step - r
                    j = column - c
                    good = (i >= 0) & (i < 3) & (j >= 0) & (j < 3) & (place == i * 24 + j * 8 + channel)
                    spread = jnp.where(good, 1.0, 0.0).astype(jnp.bfloat16)
                    at = (2 * r + c) * HID
                    first_out[3 * order + step, at : at + HID, :] = jnp.dot(
                        taps, spread, preferred_element_type=jnp.float32
                    ).astype(jnp.bfloat16)


def sweep_kernel(
    tm_count, strip_count,
    bounds_ref, factor_ref, above_ref, own_ref, below_ref, state_ref, time_weight_ref,
    wide_ref, first_ref, last_ref,
    jump_ref, sent_ref,
    rows_ref, windows_ref, velocity_ref, xa, ma, xb, mb,
):
    slice_index = lax.axis_index("tm")
    strip = lax.axis_index("strip")
    f32, bf16 = jnp.float32, jnp.bfloat16

    rows_ref[:, 0:8, :] = above_ref[...].astype(f32).reshape(8, 8, COLS)
    rows_ref[:, 8:16, :] = own_ref[...].astype(f32).reshape(8, 8, COLS)
    rows_ref[:, 16:24, :] = below_ref[...].astype(f32).reshape(8, 8, COLS)
    for window in range(3):
        for k in range(8):
            at = window * 64 + k * 8
            windows_ref[at : at + 8, :] = rows_ref[k, 2 + 6 * window : 10 + 6 * window, :]
    near = [windows_ref[64 * w : 64 * w + 64, :].astype(bf16) for w in range(3)]
    none = jnp.zeros((64, COLS), bf16)
    even = jnp.concatenate([near[0], near[1], near[2], none], axis=0)
    odd = jnp.concatenate([near[1], near[0], none, near[2]], axis=0)

    place = lax.broadcasted_iota(jnp.int32, (PAIRS, COLS), 0)
    pair = (place % LANE_ROWS) * SLABS + place // LANE_ROWS
    column = lax.broadcasted_iota(jnp.int32, (PAIRS, COLS), 1)
    picked = []
    for t in range(4):
        choose = jnp.where(column == 2 * pair + (t - 1), 1.0, 0.0).astype(bf16)
        picked.append(
            lax.dot_general(choose, odd if t % 2 else even, NT, preferred_element_type=f32)
        )
    low_half = lax.broadcasted_iota(jnp.int32, (PAIRS, 128), 1) < 64
    inputs = []
    for window in range(3):
        lanes = slice(128, 256) if window == 2 else slice(0, 128)
        lo, hi = (1, 0) if window == 1 else (0, 1)
        inputs.append(
            jnp.concatenate(
                [
                    jnp.where(low_half, picked[2 * g + lo][:, lanes], picked[2 * g + hi][:, lanes])
                    for g in range(2)
                ],
                axis=1,
            ).astype(bf16)
        )

    begin = bounds_ref[slice_index]
    finish = bounds_ref[slice_index + 1]
    time_now = jnp.full((1, 256), begin.astype(f32), f32) / STEPS
    half_bias = time_now * time_weight_ref[...] * 0.5

    lane = lax.broadcasted_iota(jnp.int32, (1, 256), 1)
    first_column = (lax.broadcasted_iota(jnp.int32, (1, 1, 256), 2) % 128) < 64

    def store(level, block, half_pre, x_out, m_out):
        blocks = 10 - level
        over = LAYERS - level
        value = half_pre * jnp.tanh(half_pre) + half_pre
        if 2 * block < over or 2 * block + 2 > 2 * blocks - over:
            row = strip * ROWS - over + 2 * block
            inside = [((row + r >= 0) & (row + r < strip_count * ROWS)).astype(f32) for r in range(2)]
            value = value * jnp.where(lane < 128, inside[0], inside[1])
        value = value.reshape(SLABS, LANE_ROWS, 256)
        edge = jnp.zeros((1, 1, 256), f32)
        after = jnp.concatenate([value[0:1, 1:], edge], axis=1)
        before = jnp.concatenate([edge, value[SLABS - 1 :, : LANE_ROWS - 1]], axis=1)
        right = jnp.concatenate([value[1:], after], axis=0)
        left = jnp.concatenate([before, value[: SLABS - 1]], axis=0)
        beside = jnp.where(first_column, right, left)
        x_out[block] = value.reshape(PAIRS, 256).astype(bf16)
        m_out[block] = beside.reshape(PAIRS, 256).astype(bf16)

    for window in range(3):
        order = 3 if window == 1 else 0
        for step in range(3):
            half_pre = lax.dot_general(
                inputs[window], first_ref[order + step], NT, preferred_element_type=f32
            )
            store(1, 3 * window + step, half_pre + half_bias, xa, ma)

    x_in, m_in, x_out, m_out = xa, ma, xb, mb
    for level in range(2, LAYERS):
        blocks = 10 - level
        for start in range(0, blocks, CHUNK):
            count = min(CHUNK, blocks - start)
            total = None
            for tile in range(4):
                source = m_in if tile // 2 else x_in
                at = start + tile % 2
                term = lax.dot_general(
                    source[at : at + count].reshape(count * PAIRS, 256),
                    wide_ref[level - 2, tile],
                    NT,
                    preferred_element_type=f32,
                )
                total = term if total is None else total + term
            for k in range(count):
                store(level, start + k, total[k * PAIRS : (k + 1) * PAIRS], x_out, m_out)
        x_in, m_in, x_out, m_out = x_out, m_out, x_in, m_in

    for block in range(4):
        total = None
        for tile in range(4):
            source = m_in if tile // 2 else x_in
            term = lax.dot_general(
                last_ref[tile], source[block + tile % 2], NT, preferred_element_type=f32
            )
            total = term if total is None else total + term
        high = total.astype(bf16)
        low = (total - high.astype(f32)).astype(bf16)
        both = None
        for c in range(2):
            spread = jnp.where(column == 2 * pair + c, 1.0, 0.0).astype(bf16)
            at = 32 * c
            for part in (high, low):
                term = jnp.dot(part[at : at + 32], spread, preferred_element_type=f32)
                both = term if both is None else both + term
        for r in range(2):
            for ch in range(4):
                at = ch * ROWS + 2 * block + r
                velocity_ref[at : at + 1, :] = both[16 * r + ch : 16 * r + ch + 1]

    time_step = jnp.full((1, COLS), (finish - begin).astype(f32), f32) / STEPS
    keeper = (slice_index != 0).astype(f32)
    jumps = []
    for ch in range(4):
        at = ch * ROWS
        state = state_ref[at : at + ROWS, :]
        fine = state + time_step * velocity_ref[at : at + ROWS, :]
        jumps.append(fine - (keeper * factor_ref[slice_index, ch]) * state)
    jump_ref[...] = jnp.concatenate(jumps, axis=0)
    passed = [jnp.float32(0.0)] * 4
    for n in range(tm_count):
        parts = []
        for ch in range(4):
            passed[ch] = jnp.where(n == slice_index, 1.0, passed[ch] * factor_ref[n, ch])
            parts.append(jnp.where(n == slice_index, 0.0, passed[ch]) * jumps[ch])
        sent_ref[n] = jnp.concatenate(parts, axis=0).astype(bf16)


def on_device(
    prev_states, observation, bounds, coarse_factor, time_weight, weight_in, weight_mid, weight_out
):
    tm_count, strip_count = lax.axis_size("tm"), lax.axis_size("strip")
    f32, bf16 = jnp.float32, jnp.bfloat16
    state = prev_states.reshape(4 * ROWS, COLS)
    features = jnp.concatenate([state.astype(bf16), observation.reshape(4 * ROWS, COLS)], axis=0)
    forward = [(i, i + 1) for i in range(strip_count - 1)]
    above = lax.ppermute(features, "strip", forward)
    below = lax.ppermute(features, "strip", [(b, a) for a, b in forward])

    vmem = pl.BlockSpec(memory_space=pltpu.VMEM)
    smem = pl.BlockSpec(memory_space=pltpu.SMEM)
    wide, first, last = pl.pallas_call(
        weights_kernel,
        out_shape=[
            jax.ShapeDtypeStruct((LAYERS - 2, 4, 256, 256), bf16),
            jax.ShapeDtypeStruct((6, 256, 256), bf16),
            jax.ShapeDtypeStruct((4, 64, 256), bf16),
        ],
        in_specs=[vmem] * 3,
        out_specs=[vmem] * 3,
        compiler_params=pltpu.CompilerParams(vmem_limit_bytes=32 * 2**20),
        cost_estimate=pl.CostEstimate(flops=10**7, bytes_accessed=4 * 10**6, transcendentals=0),
        name="weights",
    )(
        weight_mid,
        jnp.transpose(weight_in, (2, 0, 1, 3)).reshape(HID, 72),
        jnp.pad(weight_out, ((0, 0), (0, 0), (0, 12), (0, 0))),
    )
    hidden = lambda: pltpu.VMEM((10, PAIRS, 256), bf16)
    jump, sent = pl.pallas_call(
        lambda *refs: sweep_kernel(tm_count, strip_count, *refs),
        out_shape=[
            jax.ShapeDtypeStruct((4 * ROWS, COLS), f32),
            jax.ShapeDtypeStruct((tm_count, 4 * ROWS, COLS), bf16),
        ],
        in_specs=[smem, smem] + [vmem] * 8,
        out_specs=[vmem] * 2,
        scratch_shapes=[
            pltpu.VMEM((8, 24, COLS), f32),
            pltpu.VMEM((192, COLS), f32),
            pltpu.VMEM((4 * ROWS, COLS), f32),
            hidden(), hidden(), hidden(), hidden(),
        ],
        compiler_params=pltpu.CompilerParams(vmem_limit_bytes=48 * 2**20),
        cost_estimate=pl.CostEstimate(flops=4 * 10**9, bytes_accessed=4 * 10**6, transcendentals=2 * 10**6),
        name="sweep",
    )(
        bounds, coarse_factor, above, features, below, state,
        jnp.tile(time_weight, 4)[None], wide, first, last,
    )
    received = lax.all_to_all(sent, "tm", 0, 0)
    result = jump + jnp.sum(received.astype(f32), axis=0)
    return result.reshape(1, 4, ROWS, COLS)


def solution(mesh):
    placed = (P("tm", None, "strip", None), P(None, "strip", None), P(), P(), P(), P(), P(), P())
    return jax.shard_map(
        on_device,
        mesh=mesh,
        in_specs=placed,
        out_specs=P("tm", None, "strip", None),
        check_vma=False,
    )
```

```python
import jax
import jax.numpy as jnp
from jax import lax
from jax.experimental import pallas as pl
from jax.experimental.pallas import tpu as pltpu
from jax.sharding import PartitionSpec as P

LAYERS = 6
STEPS = 1000
HID = 64
ROWS = 8
COLS = 384
SLABS = 12
LANE_ROWS = 16
PAIRS = SLABS * LANE_ROWS
CHUNK = 2
NT = (((1,), (1,)), ((), ()))


def pack_kernel(state_in, seen_in, state_ref, features_ref, sems):
    state = pltpu.make_async_copy(state_in, state_ref, sems.at[0])
    seen = pltpu.make_async_copy(seen_in, features_ref.at[32:64], sems.at[1])
    state.start()
    seen.start()
    state.wait()
    features_ref[:32] = state_ref[...].astype(jnp.bfloat16)
    seen.wait()


def prepare_kernel(
    tm_count,
    bounds_in, factor_in, time_weight_in, mid_in, first_in, last_in,
    wide_ref, first_out, last_out, bias_ref, table_ref,
    bounds_ref, factor_ref, time_weight_ref, mid_ref, first_ref, last_ref, sems,
):
    f32 = jnp.float32
    copies = [
        pltpu.make_async_copy(source, target, sems.at[k])
        for k, (source, target) in enumerate(
            [
                (mid_in, mid_ref), (first_in, first_ref), (last_in, last_ref),
                (factor_in, factor_ref), (bounds_in, bounds_ref), (time_weight_in, time_weight_ref),
            ]
        )
    ]
    for copy in copies:
        copy.start()
    for copy in copies:
        copy.wait()

    def pairs_of(taps):
        zero = jnp.zeros_like(taps[0])
        join = lambda a, b: jnp.concatenate([a, b], axis=1)
        return (
            (join(taps[1], taps[2]), join(taps[0], taps[1])),
            (join(zero, taps[0]), join(taps[2], zero)),
        )

    for level in range(LAYERS - 2):
        sets = [pairs_of([mid_ref[level, i, j] * 0.5 for j in range(3)]) for i in range(3)]
        for tile in range(4):
            for r in range(2):
                for c in range(2):
                    for half in range(2):
                        i = 2 * (tile % 2) + half - r
                        block = sets[i][tile // 2][c] if 0 <= i < 3 else jnp.zeros((HID, 2 * HID), jnp.bfloat16)
                        at = (2 * r + c) * HID
                        wide_ref[level, tile, at : at + HID, 128 * half : 128 * half + 128] = block
    last = lambda i, j: jnp.concatenate([last_ref[i, j].astype(f32), jnp.zeros((12, HID), f32)], axis=0)
    sets = [pairs_of([last(i, j) for j in range(3)]) for i in range(3)]
    for tile in range(4):
        for r in range(2):
            for c in range(2):
                for half in range(2):
                    i = 2 * (tile % 2) + half - r
                    block = sets[i][tile // 2][c] if 0 <= i < 3 else jnp.zeros((16, 2 * HID), f32)
                    at = (2 * c + r) * 16
                    last_out[tile, at : at + 16, 128 * half : 128 * half + 128] = block.astype(jnp.bfloat16)
    taps = first_ref[...] * 0.5
    lane = lax.broadcasted_iota(jnp.int32, (72, 256), 1)
    place = lax.broadcasted_iota(jnp.int32, (72, 256), 0)
    channel = (lane % 64) // 8
    row = lane % 8
    for order in range(2):
        column = (lane // 64) ^ order
        for step in range(3):
            for r in range(2):
                for c in range(2):
                    i = row - 2 * step - r
                    j = column - c
                    good = (i >= 0) & (i < 3) & (j >= 0) & (j < 3) & (place == i * 24 + j * 8 + channel)
                    spread = jnp.where(good, 1.0, 0.0).astype(jnp.bfloat16)
                    at = (2 * r + c) * HID
                    first_out[3 * order + step, at : at + HID, :] = lax.dot_general(
                        taps, spread, (((0,), (0,)), ((), ())), preferred_element_type=f32
                    ).astype(jnp.bfloat16)

    slice_index = lax.axis_index("tm")
    begin = bounds_ref[slice_index]
    finish = bounds_ref[slice_index + 1]
    time_now = jnp.full((1, HID), begin.astype(f32), f32) / STEPS
    half_bias = time_now * time_weight_ref[...] * 0.5
    bias_ref[...] = jnp.concatenate([half_bias] * 4, axis=1)

    half = tm_count // 2
    odd = slice_index % 2
    last_of_pair = slice_index - odd + 1
    keeper = (slice_index != 0).astype(f32)
    for ch in range(4):
        rows = slice(ch * ROWS, (ch + 1) * ROWS)
        fill = lambda at, value: table_ref.__setitem__((at, rows, slice(None)), jnp.full((ROWS, 128), value, f32))
        passed = jnp.float32(0.0)
        for pair in range(half):
            ends = last_of_pair == 2 * pair - 1
            start = jnp.where(ends, 1.0, passed) * factor_ref[ch, 2 * pair]
            passed = start * factor_ref[ch, 2 * pair + 1]
            fill((pair + half // 2) % half, jnp.where(odd == 1, passed, start))
        fill(half, keeper * factor_ref[ch, slice_index])
        fill(half + 1, factor_ref[ch, last_of_pair])
        fill(half + 2, jnp.where(odd == 1, factor_ref[ch, slice_index], 0.0))
    table_ref[half + 3] = jnp.full((4 * ROWS, 128), (finish - begin).astype(f32), f32) / STEPS


def wide_row(table):
    return jnp.concatenate([table] * 3, axis=1)


def spread_kernel(half, pair_ref, table_ref, sent_ref, base_ref):
    odd = lax.axis_index("tm") % 2
    first, second = pair_ref[1], pair_ref[0]
    own = jnp.where(odd == 1, second, first)
    base_ref[...] = own + wide_row(table_ref[half + 2]) * first
    total = second + wide_row(table_ref[half + 1]) * first
    for at in range(half):
        sent_ref[at] = (wide_row(table_ref[at]) * total).astype(jnp.bfloat16)


def sweep_kernel(
    half, strip_count,
    above_ref, own_ref, below_ref, state_ref, wide_ref, first_ref, last_ref, bias_ref, table_ref,
    jump_ref,
    rows_ref, windows_ref, velocity_ref, xa, ma, xb, mb,
):
    strip = lax.axis_index("strip")
    f32, bf16 = jnp.float32, jnp.bfloat16

    rows_ref[:, 0:8, :] = above_ref[...].astype(f32).reshape(8, 8, COLS)
    rows_ref[:, 8:16, :] = own_ref[...].astype(f32).reshape(8, 8, COLS)
    rows_ref[:, 16:24, :] = below_ref[...].astype(f32).reshape(8, 8, COLS)
    for window in range(3):
        for k in range(8):
            at = window * 64 + k * 8
            windows_ref[at : at + 8, :] = rows_ref[k, 2 + 6 * window : 10 + 6 * window, :]
    near = [windows_ref[64 * w : 64 * w + 64, :].astype(bf16) for w in range(3)]
    none = jnp.zeros((64, COLS), bf16)
    even = jnp.concatenate([near[0], near[1], near[2], none], axis=0)
    odd = jnp.concatenate([near[1], near[0], none, near[2]], axis=0)

    place = lax.broadcasted_iota(jnp.int32, (PAIRS, COLS), 0)
    pair = (place % LANE_ROWS) * SLABS + place // LANE_ROWS
    column = lax.broadcasted_iota(jnp.int32, (PAIRS, COLS), 1)
    picked = []
    for t in range(4):
        choose = jnp.where(column == 2 * pair + (t - 1), 1.0, 0.0).astype(bf16)
        picked.append(
            lax.dot_general(choose, odd if t % 2 else even, NT, preferred_element_type=f32)
        )
    low_half = lax.broadcasted_iota(jnp.int32, (PAIRS, 128), 1) < 64
    inputs = []
    for window in range(3):
        lanes = slice(128, 256) if window == 2 else slice(0, 128)
        lo, hi = (1, 0) if window == 1 else (0, 1)
        inputs.append(
            jnp.concatenate(
                [
                    jnp.where(low_half, picked[2 * g + lo][:, lanes], picked[2 * g + hi][:, lanes])
                    for g in range(2)
                ],
                axis=1,
            ).astype(bf16)
        )

    lane = lax.broadcasted_iota(jnp.int32, (1, 256), 1)
    first_column = (lax.broadcasted_iota(jnp.int32, (1, 1, 256), 2) % 128) < 64

    def store(level, block, half_pre, x_out, m_out):
        blocks = 10 - level
        over = LAYERS - level
        value = half_pre * jnp.tanh(half_pre) + half_pre
        if 2 * block < over or 2 * block + 2 > 2 * blocks - over:
            row = strip * ROWS - over + 2 * block
            inside = [((row + r >= 0) & (row + r < strip_count * ROWS)).astype(f32) for r in range(2)]
            value = value * jnp.where(lane < 128, inside[0], inside[1])
        value = value.reshape(SLABS, LANE_ROWS, 256)
        edge = jnp.zeros((1, 1, 256), f32)
        after = jnp.concatenate([value[0:1, 1:], edge], axis=1)
        before = jnp.concatenate([edge, value[SLABS - 1 :, : LANE_ROWS - 1]], axis=1)
        right = jnp.concatenate([value[1:], after], axis=0)
        left = jnp.concatenate([before, value[: SLABS - 1]], axis=0)
        beside = jnp.where(first_column, right, left)
        x_out[block] = value.reshape(PAIRS, 256).astype(bf16)
        m_out[block] = beside.reshape(PAIRS, 256).astype(bf16)

    for window in range(3):
        order = 3 if window == 1 else 0
        for step in range(3):
            half_pre = lax.dot_general(
                inputs[window], first_ref[order + step], NT, preferred_element_type=f32
            )
            store(1, 3 * window + step, half_pre + bias_ref[...], xa, ma)

    x_in, m_in, x_out, m_out = xa, ma, xb, mb
    for level in range(2, LAYERS):
        blocks = 10 - level
        for start in range(0, blocks, CHUNK):
            count = min(CHUNK, blocks - start)
            total = None
            for tile in range(4):
                source = m_in if tile // 2 else x_in
                at = start + tile % 2
                term = lax.dot_general(
                    source[at : at + count].reshape(count * PAIRS, 256),
                    wide_ref[level - 2, tile],
                    NT,
                    preferred_element_type=f32,
                )
                total = term if total is None else total + term
            for k in range(count):
                store(level, start + k, total[k * PAIRS : (k + 1) * PAIRS], x_out, m_out)
        x_in, m_in, x_out, m_out = x_out, m_out, x_in, m_in

    for block in range(4):
        total = None
        for tile in range(4):
            source = m_in if tile // 2 else x_in
            term = lax.dot_general(
                last_ref[tile], source[block + tile % 2], NT, preferred_element_type=f32
            )
            total = term if total is None else total + term
        high = total.astype(bf16)
        low = (total - high.astype(f32)).astype(bf16)
        both = None
        for c in range(2):
            spread = jnp.where(column == 2 * pair + c, 1.0, 0.0).astype(bf16)
            at = 32 * c
            for part in (high, low):
                term = jnp.dot(part[at : at + 32], spread, preferred_element_type=f32)
                both = term if both is None else both + term
        for r in range(2):
            for ch in range(4):
                at = ch * ROWS + 2 * block + r
                velocity_ref[at : at + 1, :] = both[16 * r + ch : 16 * r + ch + 1]

    state = state_ref[...]
    fine = state + wide_row(table_ref[half + 3]) * velocity_ref[...]
    jump_ref[...] = fine - wide_row(table_ref[half]) * state


def on_device(
    prev_states, observation, bounds, coarse_factor, time_weight, weight_in, weight_mid, weight_out
):
    tm_count, strip_count = lax.axis_size("tm"), lax.axis_size("strip")
    half = tm_count // 2
    f32, bf16 = jnp.float32, jnp.bfloat16
    vmem = pl.BlockSpec(memory_space=pltpu.VMEM)
    hbm = pl.BlockSpec(memory_space=pltpu.HBM)
    shape = jax.ShapeDtypeStruct
    stay = lambda x: pltpu.with_memory_space_constraint(x, pltpu.HBM)
    state = prev_states.reshape(4 * ROWS, COLS)
    state, features = pl.pallas_call(
        pack_kernel,
        out_shape=[shape((4 * ROWS, COLS), f32), shape((64, COLS), bf16)],
        in_specs=[hbm] * 2,
        out_specs=[vmem] * 2,
        scratch_shapes=[pltpu.SemaphoreType.DMA((2,))],
        compiler_params=pltpu.CompilerParams(vmem_limit_bytes=4 * 2**20),
        name="pack",
    )(*map(stay, (state, observation.reshape(4 * ROWS, COLS))))
    forward = [(i, i + 1) for i in range(strip_count - 1)]
    above = lax.ppermute(features, "strip", forward)
    below = lax.ppermute(features, "strip", [(b, a) for a, b in forward])

    tables = pl.pallas_call(
        lambda *refs: prepare_kernel(tm_count, *refs),
        out_shape=[
            shape((LAYERS - 2, 4, 256, 256), bf16),
            shape((6, 256, 256), bf16),
            shape((4, 64, 256), bf16),
            shape((1, 256), f32),
            shape((half + 4, 4 * ROWS, 128), f32),
        ],
        in_specs=[hbm] * 6,
        out_specs=[vmem] * 5,
        scratch_shapes=[
            pltpu.SMEM(bounds.shape, jnp.int32),
            pltpu.SMEM((4, tm_count), f32),
            pltpu.VMEM((1, HID), f32),
            pltpu.VMEM(weight_mid.shape, bf16),
            pltpu.VMEM((72, HID), bf16),
            pltpu.VMEM(weight_out.shape, bf16),
            pltpu.SemaphoreType.DMA((6,)),
        ],
        compiler_params=pltpu.CompilerParams(vmem_limit_bytes=32 * 2**20),
        cost_estimate=pl.CostEstimate(flops=10**7, bytes_accessed=4 * 10**6, transcendentals=0),
        name="prepare",
    )(
        *map(
            stay,
            (
                bounds,
                coarse_factor.T,
                time_weight[None],
                weight_mid,
                jnp.transpose(weight_in, (0, 1, 3, 2)).reshape(72, HID),
                weight_out,
            ),
        )
    )
    hidden = lambda: pltpu.VMEM((10, PAIRS, 256), bf16)
    jump = pl.pallas_call(
        lambda *refs: sweep_kernel(half, strip_count, *refs),
        out_shape=shape((4 * ROWS, COLS), f32),
        in_specs=[vmem] * 9,
        out_specs=vmem,
        scratch_shapes=[
            pltpu.VMEM((8, 24, COLS), f32),
            pltpu.VMEM((192, COLS), f32),
            pltpu.VMEM((4 * ROWS, COLS), f32),
            hidden(), hidden(), hidden(), hidden(),
        ],
        compiler_params=pltpu.CompilerParams(vmem_limit_bytes=48 * 2**20),
        cost_estimate=pl.CostEstimate(flops=4 * 10**9, bytes_accessed=4 * 10**6, transcendentals=2 * 10**6),
        name="sweep",
    )(above, features, below, state, *tables)
    pair = lax.all_gather(
        jump, "tm", axis_index_groups=[[2 * p + 1, 2 * p] for p in range(half)]
    )
    sent, base = pl.pallas_call(
        lambda *refs: spread_kernel(half, *refs),
        out_shape=[shape((half, 4 * ROWS, COLS), bf16), shape((4 * ROWS, COLS), f32)],
        in_specs=[vmem] * 2,
        out_specs=[vmem] * 2,
        compiler_params=pltpu.CompilerParams(vmem_limit_bytes=4 * 2**20),
        name="spread",
    )(pair, tables[4])
    groups = [[(2 * p + half) % tm_count + j for p in range(half)] for j in range(2)]
    received = lax.all_to_all(sent, "tm", 0, 0, axis_index_groups=groups)
    result = base + jnp.sum(received.astype(f32), axis=0)
    return result.reshape(1, 4, ROWS, COLS)


def solution(mesh):
    placed = (P("tm", None, "strip", None), P(None, "strip", None), P(), P(), P(), P(), P(), P())
    return jax.shard_map(
        on_device,
        mesh=mesh,
        in_specs=placed,
        out_specs=P("tm", None, "strip", None),
        check_vma=False,
    )
```

```python
import jax
import jax.numpy as jnp
from jax import lax
from jax.experimental import pallas as pl
from jax.experimental.pallas import tpu as pltpu
from jax.sharding import PartitionSpec as P

LAYERS = 6
STEPS = 1000
HID = 64
ROWS = 8
COLS = 384
SLABS = 12
LANE_ROWS = 16
PAIRS = SLABS * LANE_ROWS
CHUNK = 2
NT = (((1,), (1,)), ((), ()))


def pack_kernel(state_in, seen_in, state_ref, features_ref, sems):
    state = pltpu.make_async_copy(state_in, state_ref, sems.at[0])
    seen = pltpu.make_async_copy(seen_in, features_ref.at[32:64], sems.at[1])
    state.start()
    seen.start()
    state.wait()
    features_ref[:32] = state_ref[...].astype(jnp.bfloat16)
    seen.wait()


def prepare_kernel(
    tm_count,
    bounds_in, factor_in, time_weight_in, mid_in, first_in, last_in,
    wide_ref, first_out, last_out, bias_ref, table_ref,
    bounds_ref, factor_ref, time_weight_ref, mid_ref, first_ref, last_ref, sems,
):
    f32 = jnp.float32
    copies = [
        pltpu.make_async_copy(source, target, sems.at[k])
        for k, (source, target) in enumerate(
            [
                (mid_in, mid_ref), (first_in, first_ref), (last_in, last_ref),
                (factor_in, factor_ref), (bounds_in, bounds_ref), (time_weight_in, time_weight_ref),
            ]
        )
    ]
    for copy in copies:
        copy.start()
    for copy in copies:
        copy.wait()

    def pairs_of(taps):
        zero = jnp.zeros_like(taps[0])
        join = lambda a, b: jnp.concatenate([a, b], axis=1)
        return (
            (join(taps[1], taps[2]), join(taps[0], taps[1])),
            (join(zero, taps[0]), join(taps[2], zero)),
        )

    for level in range(LAYERS - 2):
        sets = [pairs_of([mid_ref[level, i, j] * 0.5 for j in range(3)]) for i in range(3)]
        for tile in range(4):
            for r in range(2):
                for c in range(2):
                    for half in range(2):
                        i = 2 * (tile % 2) + half - r
                        block = sets[i][tile // 2][c] if 0 <= i < 3 else jnp.zeros((HID, 2 * HID), jnp.bfloat16)
                        at = (2 * r + c) * HID
                        wide_ref[level, tile, at : at + HID, 128 * half : 128 * half + 128] = block
    last = lambda i, j: jnp.concatenate([last_ref[i, j].astype(f32), jnp.zeros((12, HID), f32)], axis=0)
    sets = [pairs_of([last(i, j) for j in range(3)]) for i in range(3)]
    for tile in range(4):
        for r in range(2):
            for c in range(2):
                for half in range(2):
                    i = 2 * (tile % 2) + half - r
                    block = sets[i][tile // 2][c] if 0 <= i < 3 else jnp.zeros((16, 2 * HID), f32)
                    at = (2 * c + r) * 16
                    last_out[tile, at : at + 16, 128 * half : 128 * half + 128] = block.astype(jnp.bfloat16)
    taps = first_ref[...] * 0.5
    lane = lax.broadcasted_iota(jnp.int32, (72, 256), 1)
    place = lax.broadcasted_iota(jnp.int32, (72, 256), 0)
    channel = (lane % 64) // 8
    row = lane % 8
    column = lane // 64
    for step in range(3):
        for r in range(2):
            for c in range(2):
                i = row - 2 * step - r
                j = column - c
                good = (i >= 0) & (i < 3) & (j >= 0) & (j < 3) & (place == i * 24 + j * 8 + channel)
                spread = jnp.where(good, 1.0, 0.0).astype(jnp.bfloat16)
                at = (2 * r + c) * HID
                first_out[step, at : at + HID, :] = lax.dot_general(
                    taps, spread, (((0,), (0,)), ((), ())), preferred_element_type=f32
                ).astype(jnp.bfloat16)

    slice_index = lax.axis_index("tm")
    begin = bounds_ref[slice_index]
    finish = bounds_ref[slice_index + 1]
    time_now = jnp.full((1, HID), begin.astype(f32), f32) / STEPS
    half_bias = time_now * time_weight_ref[...] * 0.5
    bias_ref[...] = jnp.concatenate([half_bias] * 4, axis=1)

    half = tm_count // 2
    odd = slice_index % 2
    last_of_pair = slice_index - odd + 1
    keeper = (slice_index != 0).astype(f32)
    for ch in range(4):
        rows = slice(ch * ROWS, (ch + 1) * ROWS)
        fill = lambda at, value: table_ref.__setitem__((at, rows, slice(None)), jnp.full((ROWS, 128), value, f32))
        passed = jnp.float32(0.0)
        for pair in range(half):
            ends = last_of_pair == 2 * pair - 1
            start = jnp.where(ends, 1.0, passed) * factor_ref[ch, 2 * pair]
            passed = start * factor_ref[ch, 2 * pair + 1]
            fill((pair + half // 2) % half, jnp.where(odd == 1, passed, start))
        fill(half, keeper * factor_ref[ch, slice_index])
        fill(half + 1, factor_ref[ch, last_of_pair])
        fill(half + 2, jnp.where(odd == 1, factor_ref[ch, slice_index], 0.0))
    table_ref[half + 3] = jnp.full((4 * ROWS, 128), (finish - begin).astype(f32), f32) / STEPS


def wide_row(table):
    return jnp.concatenate([table] * 3, axis=1)


def spread_kernel(half, pair_ref, table_ref, sent_ref, base_ref):
    odd = lax.axis_index("tm") % 2
    first, second = pair_ref[1], pair_ref[0]
    own = jnp.where(odd == 1, second, first)
    base_ref[...] = own + wide_row(table_ref[half + 2]) * first
    total = second + wide_row(table_ref[half + 1]) * first
    for at in range(half):
        sent_ref[at] = (wide_row(table_ref[at]) * total).astype(jnp.bfloat16)


def sweep_kernel(
    half, strip_count,
    outer_ref, inner_ref, own_ref, state_ref, wide_ref, first_ref, last_ref, bias_ref, table_ref,
    jump_ref,
    rows_ref, windows_ref, velocity_ref, xa, ma, xb, mb,
):
    strip = lax.axis_index("strip")
    f32, bf16 = jnp.float32, jnp.bfloat16

    even_strip = strip % 2 == 0
    features = lambda value: value.astype(f32).reshape(8, 8, COLS)
    outer, own = features(outer_ref[...]), features(own_ref[...])
    inner = jnp.where(even_strip, features(inner_ref[1]), features(inner_ref[0]))
    rows_ref[:, 0:8, :] = jnp.where(even_strip, outer, inner)
    rows_ref[:, 8:16, :] = own
    rows_ref[:, 16:24, :] = jnp.where(even_strip, inner, outer)
    for window in range(3):
        for k in range(8):
            at = window * 64 + k * 8
            windows_ref[at : at + 8, :] = rows_ref[k, 2 + 6 * window : 10 + 6 * window, :]
    near = [windows_ref[64 * w : 64 * w + 64, :].astype(bf16) for w in range(3)]
    none = jnp.zeros((64, COLS), bf16)
    even = jnp.concatenate([near[0], near[1], near[2], none], axis=0)
    odd = jnp.concatenate([near[1], near[0], none, near[2]], axis=0)

    place = lax.broadcasted_iota(jnp.int32, (PAIRS, COLS), 0)
    pair = (place % LANE_ROWS) * SLABS + place // LANE_ROWS
    column = lax.broadcasted_iota(jnp.int32, (PAIRS, COLS), 1)
    choose = lambda shift: jnp.where(column == 2 * pair + shift, 1.0, 0.0).astype(bf16)
    picked = [None] * 4
    for t, rows in ((0, even), (1, odd)):
        both = lax.dot_general(
            jnp.concatenate([choose(t - 1), choose(t + 1)], axis=0), rows, NT, preferred_element_type=f32
        )
        picked[t], picked[t + 2] = both[:PAIRS], both[PAIRS:]
    low_half = lax.broadcasted_iota(jnp.int32, (PAIRS, 128), 1) < 64
    inputs = []
    for window in range(3):
        lanes = slice(128, 256) if window == 2 else slice(0, 128)
        groups = []
        for g in range(2):
            near, far = picked[2 * g][:, lanes], picked[2 * g + 1][:, lanes]
            if window == 1:
                groups.append(pltpu.roll(jnp.where(low_half, far, near), 64, 1))
            else:
                groups.append(jnp.where(low_half, near, far))
        inputs.append(jnp.concatenate(groups, axis=1).astype(bf16))
    inputs = jnp.concatenate(inputs, axis=0)

    lane = lax.broadcasted_iota(jnp.int32, (1, 256), 1)
    first_column = (lax.broadcasted_iota(jnp.int32, (1, 1, 256), 2) % 128) < 64

    def store(level, block, half_pre, x_out, m_out):
        blocks = 10 - level
        over = LAYERS - level
        value = half_pre * jnp.tanh(half_pre) + half_pre
        if 2 * block < over or 2 * block + 2 > 2 * blocks - over:
            row = strip * ROWS - over + 2 * block
            inside = [((row + r >= 0) & (row + r < strip_count * ROWS)).astype(f32) for r in range(2)]
            value = value * jnp.where(lane < 128, inside[0], inside[1])
        value = value.reshape(SLABS, LANE_ROWS, 256)
        edge = jnp.zeros((1, 1, 256), f32)
        after = jnp.concatenate([value[0:1, 1:], edge], axis=1)
        before = jnp.concatenate([edge, value[SLABS - 1 :, : LANE_ROWS - 1]], axis=1)
        right = jnp.concatenate([value[1:], after], axis=0)
        left = jnp.concatenate([before, value[: SLABS - 1]], axis=0)
        beside = jnp.where(first_column, right, left)
        x_out[block] = value.reshape(PAIRS, 256).astype(bf16)
        m_out[block] = beside.reshape(PAIRS, 256).astype(bf16)

    for step in range(3):
        half_pre = lax.dot_general(inputs, first_ref[step], NT, preferred_element_type=f32)
        for window in range(3):
            part = half_pre[window * PAIRS : (window + 1) * PAIRS]
            store(1, 3 * window + step, part + bias_ref[...], xa, ma)

    x_in, m_in, x_out, m_out = xa, ma, xb, mb
    for level in range(2, LAYERS):
        blocks = 10 - level
        for start in range(0, blocks, CHUNK):
            count = min(CHUNK, blocks - start)
            total = None
            for tile in range(4):
                source = m_in if tile // 2 else x_in
                at = start + tile % 2
                term = lax.dot_general(
                    source[at : at + count].reshape(count * PAIRS, 256),
                    wide_ref[level - 2, tile],
                    NT,
                    preferred_element_type=f32,
                )
                total = term if total is None else total + term
            for k in range(count):
                store(level, start + k, total[k * PAIRS : (k + 1) * PAIRS], x_out, m_out)
        x_in, m_in, x_out, m_out = x_out, m_out, x_in, m_in

    ends = [[], []]
    for block in range(4):
        total = None
        for tile in range(4):
            source = m_in if tile // 2 else x_in
            term = lax.dot_general(
                last_ref[tile], source[block + tile % 2], NT, preferred_element_type=f32
            )
            total = term if total is None else total + term
        high = total.astype(bf16)
        low = (total - high.astype(f32)).astype(bf16)
        for c in range(2):
            at = 32 * c
            ends[c] += [high[at : at + 32], low[at : at + 32]]
    both = None
    for c in range(2):
        term = jnp.dot(jnp.concatenate(ends[c], axis=0), choose(c), preferred_element_type=f32)
        both = term if both is None else both + term
    for block in range(4):
        at = 64 * block
        sums = both[at : at + 32] + both[at + 32 : at + 64]
        for r in range(2):
            for ch in range(4):
                at = ch * ROWS + 2 * block + r
                velocity_ref[at : at + 1, :] = sums[16 * r + ch : 16 * r + ch + 1]

    state = state_ref[...]
    fine = state + wide_row(table_ref[half + 3]) * velocity_ref[...]
    jump_ref[...] = fine - wide_row(table_ref[half]) * state


def on_device(
    prev_states, observation, bounds, coarse_factor, time_weight, weight_in, weight_mid, weight_out
):
    tm_count, strip_count = lax.axis_size("tm"), lax.axis_size("strip")
    half = tm_count // 2
    f32, bf16 = jnp.float32, jnp.bfloat16
    vmem = pl.BlockSpec(memory_space=pltpu.VMEM)
    hbm = pl.BlockSpec(memory_space=pltpu.HBM)
    shape = jax.ShapeDtypeStruct
    stay = lambda x: pltpu.with_memory_space_constraint(x, pltpu.HBM)
    state = prev_states.reshape(4 * ROWS, COLS)
    state, features = pl.pallas_call(
        pack_kernel,
        out_shape=[shape((4 * ROWS, COLS), f32), shape((64, COLS), bf16)],
        in_specs=[hbm] * 2,
        out_specs=[vmem] * 2,
        scratch_shapes=[pltpu.SemaphoreType.DMA((2,))],
        compiler_params=pltpu.CompilerParams(vmem_limit_bytes=4 * 2**20),
        name="pack",
    )(*map(stay, (state, observation.reshape(4 * ROWS, COLS))))
    swap = [
        pair for i in range(1, strip_count - 1, 2) for pair in ((i, i + 1), (i + 1, i))
    ]
    outer = lax.ppermute(features, "strip", swap)
    inner = lax.all_gather(
        features, "strip", axis_index_groups=[[i, i + 1] for i in range(0, strip_count, 2)]
    )

    tables = pl.pallas_call(
        lambda *refs: prepare_kernel(tm_count, *refs),
        out_shape=[
            shape((LAYERS - 2, 4, 256, 256), bf16),
            shape((3, 256, 256), bf16),
            shape((4, 64, 256), bf16),
            shape((1, 256), f32),
            shape((half + 4, 4 * ROWS, 128), f32),
        ],
        in_specs=[hbm] * 6,
        out_specs=[vmem] * 5,
        scratch_shapes=[
            pltpu.SMEM(bounds.shape, jnp.int32),
            pltpu.SMEM((4, tm_count), f32),
            pltpu.VMEM((1, HID), f32),
            pltpu.VMEM(weight_mid.shape, bf16),
            pltpu.VMEM((72, HID), bf16),
            pltpu.VMEM(weight_out.shape, bf16),
            pltpu.SemaphoreType.DMA((6,)),
        ],
        compiler_params=pltpu.CompilerParams(vmem_limit_bytes=32 * 2**20),
        cost_estimate=pl.CostEstimate(flops=10**7, bytes_accessed=4 * 10**6, transcendentals=0),
        name="prepare",
    )(
        *map(
            stay,
            (
                bounds,
                coarse_factor.T,
                time_weight[None],
                weight_mid,
                jnp.transpose(weight_in, (0, 1, 3, 2)).reshape(72, HID),
                weight_out,
            ),
        )
    )
    hidden = lambda: pltpu.VMEM((10, PAIRS, 256), bf16)
    jump = pl.pallas_call(
        lambda *refs: sweep_kernel(half, strip_count, *refs),
        out_shape=shape((4 * ROWS, COLS), f32),
        in_specs=[vmem] * 9,
        out_specs=vmem,
        scratch_shapes=[
            pltpu.VMEM((8, 24, COLS), f32),
            pltpu.VMEM((192, COLS), f32),
            pltpu.VMEM((4 * ROWS, COLS), f32),
            hidden(), hidden(), hidden(), hidden(),
        ],
        compiler_params=pltpu.CompilerParams(vmem_limit_bytes=48 * 2**20),
        cost_estimate=pl.CostEstimate(flops=4 * 10**9, bytes_accessed=4 * 10**6, transcendentals=2 * 10**6),
        name="sweep",
    )(outer, inner, features, state, *tables)
    pair = lax.all_gather(
        jump, "tm", axis_index_groups=[[2 * p + 1, 2 * p] for p in range(half)]
    )
    sent, base = pl.pallas_call(
        lambda *refs: spread_kernel(half, *refs),
        out_shape=[shape((half, 4 * ROWS, COLS), bf16), shape((4 * ROWS, COLS), f32)],
        in_specs=[vmem] * 2,
        out_specs=[vmem] * 2,
        compiler_params=pltpu.CompilerParams(vmem_limit_bytes=4 * 2**20),
        name="spread",
    )(pair, tables[4])
    groups = [[(2 * p + half) % tm_count + j for p in range(half)] for j in range(2)]
    received = lax.all_to_all(sent, "tm", 0, 0, axis_index_groups=groups)
    result = base + jnp.sum(received.astype(f32), axis=0)
    return result.reshape(1, 4, ROWS, COLS)


def solution(mesh):
    placed = (P("tm", None, "strip", None), P(None, "strip", None), P(), P(), P(), P(), P(), P())
    return jax.shard_map(
        on_device,
        mesh=mesh,
        in_specs=placed,
        out_specs=P("tm", None, "strip", None),
        check_vma=False,
    )
```

```python
import jax
import jax.numpy as jnp
from jax import lax
from jax.experimental import pallas as pl
from jax.experimental.pallas import tpu as pltpu
from jax.sharding import PartitionSpec as P

LAYERS = 6
STEPS = 1000
HID = 64
ROWS = 8
COLS = 384
SLABS = 12
LANE_ROWS = 16
PAIRS = SLABS * LANE_ROWS
CHUNK = 2
NT = (((1,), (1,)), ((), ()))
SHIFTS = (-1, 1, 0, 2)


def pack_kernel(state_in, seen_in, first_in, last_in, state_ref, features_ref, first_ref, last_ref, sems):
    targets = [state_ref, features_ref.at[32:64], first_ref, last_ref]
    copies = [
        pltpu.make_async_copy(source, target, sems.at[k])
        for k, (source, target) in enumerate(zip((state_in, seen_in, first_in, last_in), targets))
    ]
    for copy in copies:
        copy.start()
    copies[0].wait()
    features_ref[:32] = state_ref[...].astype(jnp.bfloat16)
    for copy in copies[1:]:
        copy.wait()


def pairs_of(taps):
    zero = jnp.zeros_like(taps[0])
    join = lambda a, b: jnp.concatenate([a, b], axis=1)
    return (
        (join(taps[1], taps[2]), join(taps[0], taps[1])),
        (join(zero, taps[0]), join(taps[2], zero)),
    )


def widen(mid_ref, wide_ref, level):
    sets = [pairs_of([mid_ref[level, i, j] * 0.5 for j in range(3)]) for i in range(3)]
    for tile in range(4):
        for r in range(2):
            for c in range(2):
                for half in range(2):
                    i = 2 * (tile % 2) + half - r
                    block = sets[i][tile // 2][c] if 0 <= i < 3 else jnp.zeros((HID, 2 * HID), jnp.bfloat16)
                    at = (2 * r + c) * HID
                    wide_ref[level, tile, at : at + HID, 128 * half : 128 * half + 128] = block


def prepare_kernel(
    tm_count,
    bounds_in, factor_in, time_weight_in, mid_in, first_ref, last_ref,
    first_out, last_out, bias_ref, table_ref, mid_ref, choose_ref,
    bounds_ref, factor_ref, time_weight_ref, sems,
):
    f32 = jnp.float32
    copies = [
        pltpu.make_async_copy(source, target, sems.at[k])
        for k, (source, target) in enumerate(
            [(mid_in, mid_ref), (factor_in, factor_ref), (bounds_in, bounds_ref), (time_weight_in, time_weight_ref)]
        )
    ]
    for copy in copies:
        copy.start()

    place = lax.broadcasted_iota(jnp.int32, (PAIRS, COLS), 0)
    pair_at = (place % LANE_ROWS) * SLABS + place // LANE_ROWS
    column = lax.broadcasted_iota(jnp.int32, (PAIRS, COLS), 1) - 2 * pair_at
    for k, shift in enumerate(SHIFTS):
        choose_ref[k * PAIRS : (k + 1) * PAIRS] = jnp.where(column == shift, 1.0, 0.0).astype(jnp.bfloat16)
    last = lambda i, j: jnp.concatenate([last_ref[i, j].astype(f32), jnp.zeros((12, HID), f32)], axis=0)
    sets = [pairs_of([last(i, j) for j in range(3)]) for i in range(3)]
    for tile in range(4):
        for r in range(2):
            for c in range(2):
                for half in range(2):
                    i = 2 * (tile % 2) + half - r
                    block = sets[i][tile // 2][c] if 0 <= i < 3 else jnp.zeros((16, 2 * HID), f32)
                    at = (2 * c + r) * 16
                    last_out[tile, at : at + 16, 128 * half : 128 * half + 128] = block.astype(jnp.bfloat16)
    taps = first_ref[...] * 0.5
    lane = lax.broadcasted_iota(jnp.int32, (72, 256), 1)
    place = lax.broadcasted_iota(jnp.int32, (72, 256), 0)
    channel = (lane % 64) // 8
    row = lane % 8
    column = lane // 64
    for step in range(3):
        for r in range(2):
            for c in range(2):
                i = row - 2 * step - r
                j = column - c
                good = (i >= 0) & (i < 3) & (j >= 0) & (j < 3) & (place == i * 24 + j * 8 + channel)
                spread = jnp.where(good, 1.0, 0.0).astype(jnp.bfloat16)
                at = (2 * r + c) * HID
                first_out[step, at : at + HID, :] = lax.dot_general(
                    taps, spread, (((0,), (0,)), ((), ())), preferred_element_type=f32
                ).astype(jnp.bfloat16)

    for copy in copies[1:]:
        copy.wait()
    slice_index = lax.axis_index("tm")
    begin = bounds_ref[slice_index]
    finish = bounds_ref[slice_index + 1]
    time_now = jnp.full((1, HID), begin.astype(f32), f32) / STEPS
    half_bias = time_now * time_weight_ref[...] * 0.5
    bias_ref[...] = jnp.concatenate([half_bias] * 4, axis=1)

    half = tm_count // 2
    odd = slice_index % 2
    last_of_pair = slice_index - odd + 1
    keeper = (slice_index != 0).astype(f32)
    for ch in range(4):
        rows = slice(ch * ROWS, (ch + 1) * ROWS)
        fill = lambda at, value: table_ref.__setitem__((at, rows, slice(None)), jnp.full((ROWS, 128), value, f32))
        passed = jnp.float32(0.0)
        for pair in range(half):
            ends = last_of_pair == 2 * pair - 1
            start = jnp.where(ends, 1.0, passed) * factor_ref[ch, 2 * pair]
            passed = start * factor_ref[ch, 2 * pair + 1]
            fill((pair + half // 2) % half, jnp.where(odd == 1, passed, start))
        fill(half, keeper * factor_ref[ch, slice_index])
        fill(half + 1, factor_ref[ch, last_of_pair])
        fill(half + 2, jnp.where(odd == 1, factor_ref[ch, slice_index], 0.0))
    table_ref[half + 3] = jnp.full((4 * ROWS, 128), (finish - begin).astype(f32), f32) / STEPS
    copies[0].wait()


def wide_row(table):
    return jnp.concatenate([table] * 3, axis=1)


def spread_kernel(half, pair_ref, table_ref, sent_ref, base_ref):
    odd = lax.axis_index("tm") % 2
    first, second = pair_ref[1], pair_ref[0]
    own = jnp.where(odd == 1, second, first)
    base_ref[...] = own + wide_row(table_ref[half + 2]) * first
    total = second + wide_row(table_ref[half + 1]) * first
    for at in range(half):
        sent_ref[at] = (wide_row(table_ref[at]) * total).astype(jnp.bfloat16)


def sweep_kernel(
    half, strip_count,
    outer_ref, inner_ref, own_ref, state_ref, first_ref, last_ref, bias_ref, table_ref, mid_ref, choose_ref,
    jump_ref,
    rows_ref, windows_ref, velocity_ref, xa, ma, xb, mb, wide_ref,
):
    strip = lax.axis_index("strip")
    f32, bf16 = jnp.float32, jnp.bfloat16

    even_strip = strip % 2 == 0
    features = lambda value: value.astype(f32).reshape(8, 8, COLS)
    outer, own = features(outer_ref[...]), features(own_ref[...])
    inner = jnp.where(even_strip, features(inner_ref[1]), features(inner_ref[0]))
    rows_ref[:, 0:8, :] = jnp.where(even_strip, outer, inner)
    rows_ref[:, 8:16, :] = own
    rows_ref[:, 16:24, :] = jnp.where(even_strip, inner, outer)
    for window in range(3):
        for k in range(8):
            at = window * 64 + k * 8
            windows_ref[at : at + 8, :] = rows_ref[k, 2 + 6 * window : 10 + 6 * window, :]
    near = [windows_ref[64 * w : 64 * w + 64, :].astype(bf16) for w in range(3)]
    none = jnp.zeros((64, COLS), bf16)
    even = jnp.concatenate([near[0], near[1], near[2], none], axis=0)
    odd = jnp.concatenate([near[1], near[0], none, near[2]], axis=0)

    picked = [None] * 4
    for t, rows in ((0, even), (1, odd)):
        both = lax.dot_general(
            choose_ref[2 * t * PAIRS : 2 * (t + 1) * PAIRS], rows, NT, preferred_element_type=f32
        )
        picked[t], picked[t + 2] = both[:PAIRS], both[PAIRS:]
    low_half = lax.broadcasted_iota(jnp.int32, (PAIRS, 128), 1) < 64
    inputs = []
    for window in range(3):
        lanes = slice(128, 256) if window == 2 else slice(0, 128)
        groups = []
        for g in range(2):
            near, far = picked[2 * g][:, lanes], picked[2 * g + 1][:, lanes]
            if window == 1:
                groups.append(pltpu.roll(jnp.where(low_half, far, near), 64, 1))
            else:
                groups.append(jnp.where(low_half, near, far))
        inputs.append(jnp.concatenate(groups, axis=1).astype(bf16))
    inputs = jnp.concatenate(inputs, axis=0)

    lane = lax.broadcasted_iota(jnp.int32, (1, 256), 1)
    first_column = (lax.broadcasted_iota(jnp.int32, (1, 1, 256), 2) % 128) < 64

    def store(level, block, half_pre, x_out, m_out):
        blocks = 10 - level
        over = LAYERS - level
        value = half_pre * jnp.tanh(half_pre) + half_pre
        if 2 * block < over or 2 * block + 2 > 2 * blocks - over:
            row = strip * ROWS - over + 2 * block
            inside = [((row + r >= 0) & (row + r < strip_count * ROWS)).astype(f32) for r in range(2)]
            value = value * jnp.where(lane < 128, inside[0], inside[1])
        value = value.reshape(SLABS, LANE_ROWS, 256)
        edge = jnp.zeros((1, 1, 256), f32)
        after = jnp.concatenate([value[0:1, 1:], edge], axis=1)
        before = jnp.concatenate([edge, value[SLABS - 1 :, : LANE_ROWS - 1]], axis=1)
        right = jnp.concatenate([value[1:], after], axis=0)
        left = jnp.concatenate([before, value[: SLABS - 1]], axis=0)
        beside = jnp.where(first_column, right, left)
        x_out[block] = value.reshape(PAIRS, 256).astype(bf16)
        m_out[block] = beside.reshape(PAIRS, 256).astype(bf16)

    widen(mid_ref, wide_ref, 0)
    for step in range(3):
        half_pre = lax.dot_general(inputs, first_ref[step], NT, preferred_element_type=f32)
        for window in range(3):
            part = half_pre[window * PAIRS : (window + 1) * PAIRS]
            store(1, 3 * window + step, part + bias_ref[...], xa, ma)

    x_in, m_in, x_out, m_out = xa, ma, xb, mb
    for level in range(2, LAYERS):
        blocks = 10 - level
        if level < LAYERS - 1:
            widen(mid_ref, wide_ref, level - 1)
        for start in range(0, blocks, CHUNK):
            count = min(CHUNK, blocks - start)
            total = None
            for tile in range(4):
                source = m_in if tile // 2 else x_in
                at = start + tile % 2
                term = lax.dot_general(
                    source[at : at + count].reshape(count * PAIRS, 256),
                    wide_ref[level - 2, tile],
                    NT,
                    preferred_element_type=f32,
                )
                total = term if total is None else total + term
            for k in range(count):
                store(level, start + k, total[k * PAIRS : (k + 1) * PAIRS], x_out, m_out)
        x_in, m_in, x_out, m_out = x_out, m_out, x_in, m_in

    ends = [[], []]
    for block in range(4):
        total = None
        for tile in range(4):
            source = m_in if tile // 2 else x_in
            term = lax.dot_general(
                last_ref[tile], source[block + tile % 2], NT, preferred_element_type=f32
            )
            total = term if total is None else total + term
        high = total.astype(bf16)
        low = (total - high.astype(f32)).astype(bf16)
        for c in range(2):
            at = 32 * c
            ends[c] += [high[at : at + 32], low[at : at + 32]]
    both = None
    for c in range(2):
        at = SHIFTS.index(c) * PAIRS
        term = jnp.dot(jnp.concatenate(ends[c], axis=0), choose_ref[at : at + PAIRS], preferred_element_type=f32)
        both = term if both is None else both + term
    for block in range(4):
        at = 64 * block
        sums = both[at : at + 32] + both[at + 32 : at + 64]
        for r in range(2):
            for ch in range(4):
                at = ch * ROWS + 2 * block + r
                velocity_ref[at : at + 1, :] = sums[16 * r + ch : 16 * r + ch + 1]

    state = state_ref[...]
    fine = state + wide_row(table_ref[half + 3]) * velocity_ref[...]
    jump_ref[...] = fine - wide_row(table_ref[half]) * state


def on_device(
    prev_states, observation, bounds, coarse_factor, time_weight, weight_in, weight_mid, weight_out
):
    tm_count, strip_count = lax.axis_size("tm"), lax.axis_size("strip")
    half = tm_count // 2
    f32, bf16 = jnp.float32, jnp.bfloat16
    vmem = pl.BlockSpec(memory_space=pltpu.VMEM)
    hbm = pl.BlockSpec(memory_space=pltpu.HBM)
    shape = jax.ShapeDtypeStruct
    stay = lambda x: pltpu.with_memory_space_constraint(x, pltpu.HBM)
    state = prev_states.reshape(4 * ROWS, COLS)
    taps = jnp.transpose(weight_in, (0, 1, 3, 2)).reshape(72, HID)
    state, features, first, last = pl.pallas_call(
        pack_kernel,
        out_shape=[
            shape((4 * ROWS, COLS), f32),
            shape((64, COLS), bf16),
            shape(taps.shape, bf16),
            shape(weight_out.shape, bf16),
        ],
        in_specs=[hbm] * 4,
        out_specs=[vmem] * 4,
        scratch_shapes=[pltpu.SemaphoreType.DMA((4,))],
        compiler_params=pltpu.CompilerParams(vmem_limit_bytes=4 * 2**20),
        name="pack",
    )(*map(stay, (state, observation.reshape(4 * ROWS, COLS), taps, weight_out)))
    swap = [
        pair for i in range(1, strip_count - 1, 2) for pair in ((i, i + 1), (i + 1, i))
    ]
    outer = lax.ppermute(features, "strip", swap)
    inner = lax.all_gather(
        features, "strip", axis_index_groups=[[i, i + 1] for i in range(0, strip_count, 2)]
    )

    tables = pl.pallas_call(
        lambda *refs: prepare_kernel(tm_count, *refs),
        out_shape=[
            shape((3, 256, 256), bf16),
            shape((4, 64, 256), bf16),
            shape((1, 256), f32),
            shape((half + 4, 4 * ROWS, 128), f32),
            shape(weight_mid.shape, bf16),
            shape((4 * PAIRS, COLS), bf16),
        ],
        in_specs=[hbm] * 4 + [vmem] * 2,
        out_specs=[vmem] * 6,
        scratch_shapes=[
            pltpu.SMEM(bounds.shape, jnp.int32),
            pltpu.SMEM((4, tm_count), f32),
            pltpu.VMEM((1, HID), f32),
            pltpu.SemaphoreType.DMA((4,)),
        ],
        compiler_params=pltpu.CompilerParams(vmem_limit_bytes=32 * 2**20),
        cost_estimate=pl.CostEstimate(flops=10**7, bytes_accessed=4 * 10**6, transcendentals=0),
        name="prepare",
    )(*map(stay, (bounds, coarse_factor.T, time_weight[None], weight_mid)), first, last)
    hidden = lambda: pltpu.VMEM((10, PAIRS, 256), bf16)
    jump = pl.pallas_call(
        lambda *refs: sweep_kernel(half, strip_count, *refs),
        out_shape=shape((4 * ROWS, COLS), f32),
        in_specs=[vmem] * 10,
        out_specs=vmem,
        scratch_shapes=[
            pltpu.VMEM((8, 24, COLS), f32),
            pltpu.VMEM((192, COLS), f32),
            pltpu.VMEM((4 * ROWS, COLS), f32),
            hidden(), hidden(), hidden(), hidden(),
            pltpu.VMEM((LAYERS - 2, 4, 256, 256), bf16),
        ],
        compiler_params=pltpu.CompilerParams(vmem_limit_bytes=48 * 2**20),
        cost_estimate=pl.CostEstimate(flops=4 * 10**9, bytes_accessed=4 * 10**6, transcendentals=2 * 10**6),
        name="sweep",
    )(outer, inner, features, state, *tables)
    pair = lax.all_gather(
        jump, "tm", axis_index_groups=[[2 * p + 1, 2 * p] for p in range(half)]
    )
    sent, base = pl.pallas_call(
        lambda *refs: spread_kernel(half, *refs),
        out_shape=[shape((half, 4 * ROWS, COLS), bf16), shape((4 * ROWS, COLS), f32)],
        in_specs=[vmem] * 2,
        out_specs=[vmem] * 2,
        compiler_params=pltpu.CompilerParams(vmem_limit_bytes=4 * 2**20),
        name="spread",
    )(pair, tables[3])
    groups = [[(2 * p + half) % tm_count + j for p in range(half)] for j in range(2)]
    received = lax.all_to_all(sent, "tm", 0, 0, axis_index_groups=groups)
    result = base + jnp.sum(received.astype(f32), axis=0)
    return result.reshape(1, 4, ROWS, COLS)


def solution(mesh):
    placed = (P("tm", None, "strip", None), P(None, "strip", None), P(), P(), P(), P(), P(), P())
    return jax.shard_map(
        on_device,
        mesh=mesh,
        in_specs=placed,
        out_specs=P("tm", None, "strip", None),
        check_vma=False,
    )
```

```python
import jax
import jax.numpy as jnp
from jax import lax
from jax.experimental import pallas as pl
from jax.experimental.pallas import tpu as pltpu
from jax.sharding import PartitionSpec as P

LAYERS = 6
STEPS = 1000
HID = 64
ROWS = 8
COLS = 384
SLABS = 12
LANE_ROWS = 16
PAIRS = SLABS * LANE_ROWS
CHUNK = 2
NT = (((1,), (1,)), ((), ()))
SHIFTS = (-1, 1, 0, 2)


def pack_kernel(state_in, seen_in, state_ref, features_ref, sems):
    targets = [state_ref, features_ref.at[32:64]]
    copies = [
        pltpu.make_async_copy(source, target, sems.at[k])
        for k, (source, target) in enumerate(zip((state_in, seen_in), targets))
    ]
    for copy in copies:
        copy.start()
    copies[0].wait()
    features_ref[:32] = state_ref[...].astype(jnp.bfloat16)
    for copy in copies[1:]:
        copy.wait()


def pairs_of(taps):
    zero = jnp.zeros_like(taps[0])
    join = lambda a, b: jnp.concatenate([a, b], axis=1)
    return (
        (join(taps[1], taps[2]), join(taps[0], taps[1])),
        (join(zero, taps[0]), join(taps[2], zero)),
    )


def widen(mid_ref, wide_ref, level):
    sets = [pairs_of([mid_ref[level, i, j] * 0.5 for j in range(3)]) for i in range(3)]
    for tile in range(4):
        for r in range(2):
            for c in range(2):
                for half in range(2):
                    i = 2 * (tile % 2) + half - r
                    block = sets[i][tile // 2][c] if 0 <= i < 3 else jnp.zeros((HID, 2 * HID), jnp.bfloat16)
                    at = (2 * r + c) * HID
                    wide_ref[level, tile, at : at + HID, 128 * half : 128 * half + 128] = block


def prepare_kernel(
    tm_count,
    bounds_in, factor_in, time_weight_in, mid_in, first_ref, last_ref,
    first_out, last_out, bias_ref, table_ref, mid_ref, choose_ref,
    bounds_ref, factor_ref, time_weight_ref, sems,
):
    f32 = jnp.float32
    copies = [
        pltpu.make_async_copy(source, target, sems.at[k])
        for k, (source, target) in enumerate(
            [(mid_in, mid_ref), (factor_in, factor_ref), (bounds_in, bounds_ref), (time_weight_in, time_weight_ref)]
        )
    ]
    for copy in copies:
        copy.start()

    place = lax.broadcasted_iota(jnp.int32, (PAIRS, COLS), 0)
    pair_at = (place % LANE_ROWS) * SLABS + place // LANE_ROWS
    column = lax.broadcasted_iota(jnp.int32, (PAIRS, COLS), 1) - 2 * pair_at
    for k, shift in enumerate(SHIFTS):
        choose_ref[k * PAIRS : (k + 1) * PAIRS] = jnp.where(column == shift, 1.0, 0.0).astype(jnp.bfloat16)
    last = lambda i, j: jnp.concatenate([last_ref[i, j].astype(f32), jnp.zeros((12, HID), f32)], axis=0)
    sets = [pairs_of([last(i, j) for j in range(3)]) for i in range(3)]
    for tile in range(4):
        for r in range(2):
            for c in range(2):
                for half in range(2):
                    i = 2 * (tile % 2) + half - r
                    block = sets[i][tile // 2][c] if 0 <= i < 3 else jnp.zeros((16, 2 * HID), f32)
                    at = (2 * c + r) * 16
                    last_out[tile, at : at + 16, 128 * half : 128 * half + 128] = block.astype(jnp.bfloat16)
    taps = first_ref[...] * 0.5
    lane = lax.broadcasted_iota(jnp.int32, (72, 256), 1)
    place = lax.broadcasted_iota(jnp.int32, (72, 256), 0)
    channel = (lane % 64) // 8
    row = lane % 8
    column = lane // 64
    for step in range(3):
        for r in range(2):
            for c in range(2):
                i = row - 2 * step - r
                j = column - c
                good = (i >= 0) & (i < 3) & (j >= 0) & (j < 3) & (place == i * 24 + j * 8 + channel)
                spread = jnp.where(good, 1.0, 0.0).astype(jnp.bfloat16)
                at = (2 * r + c) * HID
                first_out[step, at : at + HID, :] = lax.dot_general(
                    taps, spread, (((0,), (0,)), ((), ())), preferred_element_type=f32
                ).astype(jnp.bfloat16)

    for copy in copies[1:]:
        copy.wait()
    slice_index = lax.axis_index("tm")
    begin = bounds_ref[slice_index]
    finish = bounds_ref[slice_index + 1]
    time_now = jnp.full((1, HID), begin.astype(f32), f32) / STEPS
    half_bias = time_now * time_weight_ref[...] * 0.5
    bias_ref[...] = jnp.concatenate([half_bias] * 4, axis=1)

    half = tm_count // 2
    odd = slice_index % 2
    last_of_pair = slice_index - odd + 1
    keeper = (slice_index != 0).astype(f32)
    for ch in range(4):
        rows = slice(ch * ROWS, (ch + 1) * ROWS)
        fill = lambda at, value: table_ref.__setitem__((at, rows, slice(None)), jnp.full((ROWS, 128), value, f32))
        passed = jnp.float32(0.0)
        for pair in range(half):
            ends = last_of_pair == 2 * pair - 1
            start = jnp.where(ends, 1.0, passed) * factor_ref[ch, 2 * pair]
            passed = start * factor_ref[ch, 2 * pair + 1]
            fill((pair + half // 2) % half, jnp.where(odd == 1, passed, start))
        fill(half, keeper * factor_ref[ch, slice_index])
        fill(half + 1, factor_ref[ch, last_of_pair])
        fill(half + 2, jnp.where(odd == 1, factor_ref[ch, slice_index], 0.0))
    table_ref[half + 3] = jnp.full((4 * ROWS, 128), (finish - begin).astype(f32), f32) / STEPS
    copies[0].wait()


def wide_row(table):
    return jnp.concatenate([table] * 3, axis=1)


def spread_kernel(half, pair_ref, table_ref, sent_ref, base_ref):
    odd = lax.axis_index("tm") % 2
    first, second = pair_ref[1], pair_ref[0]
    own = jnp.where(odd == 1, second, first)
    base_ref[...] = own + wide_row(table_ref[half + 2]) * first
    total = second + wide_row(table_ref[half + 1]) * first
    for at in range(half):
        sent_ref[at] = (wide_row(table_ref[at]) * total).astype(jnp.bfloat16)


def sweep_kernel(
    half, strip_count,
    outer_ref, inner_ref, own_ref, state_ref, first_ref, last_ref, bias_ref, table_ref, mid_ref, choose_ref,
    jump_ref,
    rows_ref, windows_ref, velocity_ref, xa, ma, xb, mb, wide_ref,
):
    strip = lax.axis_index("strip")
    f32, bf16 = jnp.float32, jnp.bfloat16

    even_strip = strip % 2 == 0
    features = lambda value: value.astype(f32).reshape(8, 8, COLS)
    outer, own = features(outer_ref[...]), features(own_ref[...])
    inner = jnp.where(even_strip, features(inner_ref[1]), features(inner_ref[0]))
    rows_ref[:, 0:8, :] = jnp.where(even_strip, outer, inner)
    rows_ref[:, 8:16, :] = own
    rows_ref[:, 16:24, :] = jnp.where(even_strip, inner, outer)
    for window in range(3):
        for k in range(8):
            at = window * 64 + k * 8
            windows_ref[at : at + 8, :] = rows_ref[k, 2 + 6 * window : 10 + 6 * window, :]
    near = [windows_ref[64 * w : 64 * w + 64, :].astype(bf16) for w in range(3)]
    none = jnp.zeros((64, COLS), bf16)
    even = jnp.concatenate([near[0], near[1], near[2], none], axis=0)
    odd = jnp.concatenate([near[1], near[0], none, near[2]], axis=0)

    picked = [None] * 4
    for t, rows in ((0, even), (1, odd)):
        both = lax.dot_general(
            choose_ref[2 * t * PAIRS : 2 * (t + 1) * PAIRS], rows, NT, preferred_element_type=f32
        )
        picked[t], picked[t + 2] = both[:PAIRS], both[PAIRS:]
    low_half = lax.broadcasted_iota(jnp.int32, (PAIRS, 128), 1) < 64
    inputs = []
    for window in range(3):
        lanes = slice(128, 256) if window == 2 else slice(0, 128)
        groups = []
        for g in range(2):
            near, far = picked[2 * g][:, lanes], picked[2 * g + 1][:, lanes]
            if window == 1:
                groups.append(pltpu.roll(jnp.where(low_half, far, near), 64, 1))
            else:
                groups.append(jnp.where(low_half, near, far))
        inputs.append(jnp.concatenate(groups, axis=1).astype(bf16))
    inputs = jnp.concatenate(inputs, axis=0)

    lane = lax.broadcasted_iota(jnp.int32, (1, 256), 1)
    first_column = (lax.broadcasted_iota(jnp.int32, (1, 1, 256), 2) % 128) < 64

    def store(level, block, half_pre, x_out, m_out):
        blocks = 10 - level
        over = LAYERS - level
        value = half_pre * jnp.tanh(half_pre) + half_pre
        if 2 * block < over or 2 * block + 2 > 2 * blocks - over:
            row = strip * ROWS - over + 2 * block
            inside = [((row + r >= 0) & (row + r < strip_count * ROWS)).astype(f32) for r in range(2)]
            value = value * jnp.where(lane < 128, inside[0], inside[1])
        value = value.reshape(SLABS, LANE_ROWS, 256)
        edge = jnp.zeros((1, 1, 256), f32)
        after = jnp.concatenate([value[0:1, 1:], edge], axis=1)
        before = jnp.concatenate([edge, value[SLABS - 1 :, : LANE_ROWS - 1]], axis=1)
        right = jnp.concatenate([value[1:], after], axis=0)
        left = jnp.concatenate([before, value[: SLABS - 1]], axis=0)
        beside = jnp.where(first_column, right, left)
        x_out[block] = value.reshape(PAIRS, 256).astype(bf16)
        m_out[block] = beside.reshape(PAIRS, 256).astype(bf16)

    widen(mid_ref, wide_ref, 0)
    for step in range(3):
        half_pre = lax.dot_general(inputs, first_ref[step], NT, preferred_element_type=f32)
        for window in range(3):
            part = half_pre[window * PAIRS : (window + 1) * PAIRS]
            store(1, 3 * window + step, part + bias_ref[...], xa, ma)

    x_in, m_in, x_out, m_out = xa, ma, xb, mb
    for level in range(2, LAYERS):
        blocks = 10 - level
        if level < LAYERS - 1:
            widen(mid_ref, wide_ref, level - 1)
        for start in range(0, blocks, CHUNK):
            count = min(CHUNK, blocks - start)
            total = None
            for tile in range(4):
                source = m_in if tile // 2 else x_in
                at = start + tile % 2
                term = lax.dot_general(
                    source[at : at + count].reshape(count * PAIRS, 256),
                    wide_ref[level - 2, tile],
                    NT,
                    preferred_element_type=f32,
                )
                total = term if total is None else total + term
            for k in range(count):
                store(level, start + k, total[k * PAIRS : (k + 1) * PAIRS], x_out, m_out)
        x_in, m_in, x_out, m_out = x_out, m_out, x_in, m_in

    ends = [[], []]
    for block in range(4):
        total = None
        for tile in range(4):
            source = m_in if tile // 2 else x_in
            term = lax.dot_general(
                last_ref[tile], source[block + tile % 2], NT, preferred_element_type=f32
            )
            total = term if total is None else total + term
        high = total.astype(bf16)
        low = (total - high.astype(f32)).astype(bf16)
        for c in range(2):
            at = 32 * c
            ends[c] += [high[at : at + 32], low[at : at + 32]]
    both = None
    for c in range(2):
        at = SHIFTS.index(c) * PAIRS
        term = jnp.dot(jnp.concatenate(ends[c], axis=0), choose_ref[at : at + PAIRS], preferred_element_type=f32)
        both = term if both is None else both + term
    for block in range(4):
        at = 64 * block
        sums = both[at : at + 32] + both[at + 32 : at + 64]
        for r in range(2):
            for ch in range(4):
                at = ch * ROWS + 2 * block + r
                velocity_ref[at : at + 1, :] = sums[16 * r + ch : 16 * r + ch + 1]

    state = state_ref[...]
    fine = state + wide_row(table_ref[half + 3]) * velocity_ref[...]
    jump_ref[...] = fine - wide_row(table_ref[half]) * state


def on_device(
    prev_states, observation, bounds, coarse_factor, time_weight, weight_in, weight_mid, weight_out
):
    tm_count, strip_count = lax.axis_size("tm"), lax.axis_size("strip")
    half = tm_count // 2
    f32, bf16 = jnp.float32, jnp.bfloat16
    vmem = pl.BlockSpec(memory_space=pltpu.VMEM)
    hbm = pl.BlockSpec(memory_space=pltpu.HBM)
    shape = jax.ShapeDtypeStruct
    stay = lambda x: pltpu.with_memory_space_constraint(x, pltpu.HBM)
    state = prev_states.reshape(4 * ROWS, COLS)
    taps = jnp.transpose(weight_in, (0, 1, 3, 2)).reshape(72, HID)
    state, features = pl.pallas_call(
        pack_kernel,
        out_shape=[
            shape((4 * ROWS, COLS), f32),
            shape((64, COLS), bf16),
        ],
        in_specs=[hbm] * 2,
        out_specs=[vmem] * 2,
        scratch_shapes=[pltpu.SemaphoreType.DMA((2,))],
        compiler_params=pltpu.CompilerParams(vmem_limit_bytes=4 * 2**20),
        name="pack",
    )(*map(stay, (state, observation.reshape(4 * ROWS, COLS))))
    swap = [
        pair for i in range(1, strip_count - 1, 2) for pair in ((i, i + 1), (i + 1, i))
    ]
    outer = lax.ppermute(features, "strip", swap)
    inner = lax.all_gather(
        features, "strip", axis_index_groups=[[i, i + 1] for i in range(0, strip_count, 2)]
    )

    tables = pl.pallas_call(
        lambda *refs: prepare_kernel(tm_count, *refs),
        out_shape=[
            shape((3, 256, 256), bf16),
            shape((4, 64, 256), bf16),
            shape((1, 256), f32),
            shape((half + 4, 4 * ROWS, 128), f32),
            shape(weight_mid.shape, bf16),
            shape((4 * PAIRS, COLS), bf16),
        ],
        in_specs=[hbm] * 4 + [vmem] * 2,
        out_specs=[vmem] * 6,
        scratch_shapes=[
            pltpu.SMEM(bounds.shape, jnp.int32),
            pltpu.SMEM((4, tm_count), f32),
            pltpu.VMEM((1, HID), f32),
            pltpu.SemaphoreType.DMA((4,)),
        ],
        compiler_params=pltpu.CompilerParams(vmem_limit_bytes=32 * 2**20),
        cost_estimate=pl.CostEstimate(flops=10**7, bytes_accessed=4 * 10**6, transcendentals=0),
        name="prepare",
    )(*map(stay, (bounds, coarse_factor.T, time_weight[None], weight_mid, taps, weight_out)))
    hidden = lambda: pltpu.VMEM((10, PAIRS, 256), bf16)
    jump = pl.pallas_call(
        lambda *refs: sweep_kernel(half, strip_count, *refs),
        out_shape=shape((4 * ROWS, COLS), f32),
        in_specs=[vmem] * 10,
        out_specs=vmem,
        scratch_shapes=[
            pltpu.VMEM((8, 24, COLS), f32),
            pltpu.VMEM((192, COLS), f32),
            pltpu.VMEM((4 * ROWS, COLS), f32),
            hidden(), hidden(), hidden(), hidden(),
            pltpu.VMEM((LAYERS - 2, 4, 256, 256), bf16),
        ],
        compiler_params=pltpu.CompilerParams(vmem_limit_bytes=48 * 2**20),
        cost_estimate=pl.CostEstimate(flops=4 * 10**9, bytes_accessed=4 * 10**6, transcendentals=2 * 10**6),
        name="sweep",
    )(outer, inner, features, state, *tables)
    pair = lax.all_gather(
        jump, "tm", axis_index_groups=[[2 * p + 1, 2 * p] for p in range(half)]
    )
    sent, base = pl.pallas_call(
        lambda *refs: spread_kernel(half, *refs),
        out_shape=[shape((half, 4 * ROWS, COLS), bf16), shape((4 * ROWS, COLS), f32)],
        in_specs=[vmem] * 2,
        out_specs=[vmem] * 2,
        compiler_params=pltpu.CompilerParams(vmem_limit_bytes=4 * 2**20),
        name="spread",
    )(pair, tables[3])
    groups = [[(2 * p + half) % tm_count + j for p in range(half)] for j in range(2)]
    received = lax.all_to_all(sent, "tm", 0, 0, axis_index_groups=groups)
    result = base + jnp.sum(received.astype(f32), axis=0)
    return result.reshape(1, 4, ROWS, COLS)


def solution(mesh):
    placed = (P("tm", None, "strip", None), P(None, "strip", None), P(), P(), P(), P(), P(), P())
    return jax.shard_map(
        on_device,
        mesh=mesh,
        in_specs=placed,
        out_specs=P("tm", None, "strip", None),
        check_vma=False,
    )
```

```python
import jax
import jax.numpy as jnp
from jax import lax
from jax.experimental import pallas as pl
from jax.experimental.pallas import tpu as pltpu
from jax.sharding import PartitionSpec as P

LAYERS = 6
STEPS = 1000
HID = 64
ROWS = 8
COLS = 384
SLABS = 12
LANE_ROWS = 16
PAIRS = SLABS * LANE_ROWS
CHUNK = 2
NT = (((1,), (1,)), ((), ()))
SHIFTS = (-1, 1, 0, 2)


def pack_kernel(state_in, seen_in, state_ref, features_ref, sems):
    targets = [state_ref, features_ref.at[32:64]]
    copies = [
        pltpu.make_async_copy(source, target, sems.at[k])
        for k, (source, target) in enumerate(zip((state_in, seen_in), targets))
    ]
    for copy in copies:
        copy.start()
    copies[0].wait()
    features_ref[:32] = state_ref[...].astype(jnp.bfloat16)
    for copy in copies[1:]:
        copy.wait()


def pairs_of(taps):
    zero = jnp.zeros_like(taps[0])
    join = lambda a, b: jnp.concatenate([a, b], axis=1)
    return (
        (join(taps[1], taps[2]), join(taps[0], taps[1])),
        (join(zero, taps[0]), join(taps[2], zero)),
    )


def widen(mid_ref, wide_ref, level):
    sets = [pairs_of([mid_ref[level, i, j] * 0.5 for j in range(3)]) for i in range(3)]
    for tile in range(4):
        for r in range(2):
            for c in range(2):
                for half in range(2):
                    i = 2 * (tile % 2) + half - r
                    block = sets[i][tile // 2][c] if 0 <= i < 3 else jnp.zeros((HID, 2 * HID), jnp.bfloat16)
                    at = (2 * r + c) * HID
                    wide_ref[level, tile, at : at + HID, 128 * half : 128 * half + 128] = block


def prepare_kernel(
    tm_count,
    bounds_in, factor_in, time_weight_in, mid_in, first_ref, last_ref,
    first_out, last_out, bias_ref, table_ref, mid_ref, choose_ref,
    bounds_ref, factor_ref, time_weight_ref, sems,
):
    f32 = jnp.float32
    copies = [
        pltpu.make_async_copy(source, target, sems.at[k])
        for k, (source, target) in enumerate(
            [(mid_in, mid_ref), (factor_in, factor_ref), (bounds_in, bounds_ref), (time_weight_in, time_weight_ref)]
        )
    ]
    for copy in copies:
        copy.start()

    place = lax.broadcasted_iota(jnp.int32, (PAIRS, COLS), 0)
    pair_at = (place % LANE_ROWS) * SLABS + place // LANE_ROWS
    column = lax.broadcasted_iota(jnp.int32, (PAIRS, COLS), 1) - 2 * pair_at
    for k, shift in enumerate(SHIFTS):
        choose_ref[k * PAIRS : (k + 1) * PAIRS] = jnp.where(column == shift, 1.0, 0.0).astype(jnp.bfloat16)
    last = lambda i, j: jnp.concatenate([last_ref[i, j].astype(f32), jnp.zeros((12, HID), f32)], axis=0)
    sets = [pairs_of([last(i, j) for j in range(3)]) for i in range(3)]
    for tile in range(4):
        for r in range(2):
            for c in range(2):
                for half in range(2):
                    i = 2 * (tile % 2) + half - r
                    block = sets[i][tile // 2][c] if 0 <= i < 3 else jnp.zeros((16, 2 * HID), f32)
                    at = (2 * c + r) * 16
                    last_out[tile, at : at + 16, 128 * half : 128 * half + 128] = block.astype(jnp.bfloat16)
    taps = first_ref[...] * 0.5
    lane = lax.broadcasted_iota(jnp.int32, (72, 256), 1)
    place = lax.broadcasted_iota(jnp.int32, (72, 256), 0)
    channel = (lane % 64) // 8
    row = lane % 8
    column = lane // 64
    for step in range(3):
        for r in range(2):
            for c in range(2):
                i = row - 2 * step - r
                j = column - c
                good = (i >= 0) & (i < 3) & (j >= 0) & (j < 3) & (place == i * 24 + j * 8 + channel)
                spread = jnp.where(good, 1.0, 0.0).astype(jnp.bfloat16)
                at = (2 * r + c) * HID
                first_out[step, at : at + HID, :] = lax.dot_general(
                    taps, spread, (((0,), (0,)), ((), ())), preferred_element_type=f32
                ).astype(jnp.bfloat16)

    for copy in copies[1:]:
        copy.wait()
    slice_index = lax.axis_index("tm")
    begin = bounds_ref[slice_index]
    finish = bounds_ref[slice_index + 1]
    time_now = jnp.full((1, HID), begin.astype(f32), f32) / STEPS
    half_bias = time_now * time_weight_ref[...] * 0.5
    bias_ref[...] = jnp.concatenate([half_bias] * 4, axis=1)

    half = tm_count // 2
    odd = slice_index % 2
    last_of_pair = slice_index - odd + 1
    keeper = (slice_index != 0).astype(f32)
    for ch in range(4):
        rows = slice(ch * ROWS, (ch + 1) * ROWS)
        fill = lambda at, value: table_ref.__setitem__((at, rows, slice(None)), jnp.full((ROWS, 128), value, f32))
        passed = jnp.float32(0.0)
        for pair in range(half):
            ends = last_of_pair == 2 * pair - 1
            start = jnp.where(ends, 1.0, passed) * factor_ref[ch, 2 * pair]
            passed = start * factor_ref[ch, 2 * pair + 1]
            fill((pair - half // 2 - 1) % half, jnp.where(odd == 1, passed, start))
        fill(half, keeper * factor_ref[ch, slice_index])
        fill(half + 1, factor_ref[ch, last_of_pair])
        fill(half + 2, jnp.where(odd == 1, factor_ref[ch, slice_index], 0.0))
    table_ref[half + 3] = jnp.full((4 * ROWS, 128), (finish - begin).astype(f32), f32) / STEPS
    copies[0].wait()


def wide_row(table):
    return jnp.concatenate([table] * 3, axis=1)


def spread_kernel(half, pair_ref, table_ref, sent_ref, base_ref):
    odd = lax.axis_index("tm") % 2
    first, second = pair_ref[1], pair_ref[0]
    own = jnp.where(odd == 1, second, first)
    base_ref[...] = own + wide_row(table_ref[half + 2]) * first
    total = second + wide_row(table_ref[half + 1]) * first
    for at in range(half):
        sent_ref[at] = (wide_row(table_ref[at]) * total).astype(jnp.bfloat16)


def sweep_kernel(
    half, strip_count,
    outer_ref, inner_ref, own_ref, state_ref, first_ref, last_ref, bias_ref, table_ref, mid_ref, choose_ref,
    jump_ref,
    rows_ref, windows_ref, velocity_ref, xa, ma, xb, mb, wide_ref,
):
    strip = lax.axis_index("strip")
    f32, bf16 = jnp.float32, jnp.bfloat16

    even_strip = strip % 2 == 0
    features = lambda value: value.astype(f32).reshape(8, 8, COLS)
    outer, own = features(outer_ref[...]), features(own_ref[...])
    inner = jnp.where(even_strip, features(inner_ref[1]), features(inner_ref[0]))
    rows_ref[:, 0:8, :] = jnp.where(even_strip, outer, inner)
    rows_ref[:, 8:16, :] = own
    rows_ref[:, 16:24, :] = jnp.where(even_strip, inner, outer)
    for window in range(3):
        for k in range(8):
            at = window * 64 + k * 8
            windows_ref[at : at + 8, :] = rows_ref[k, 2 + 6 * window : 10 + 6 * window, :]
    near = [windows_ref[64 * w : 64 * w + 64, :].astype(bf16) for w in range(3)]
    none = jnp.zeros((64, COLS), bf16)
    even = jnp.concatenate([near[0], near[1], near[2], none], axis=0)
    odd = jnp.concatenate([near[1], near[0], none, near[2]], axis=0)

    picked = [None] * 4
    for t, rows in ((0, even), (1, odd)):
        both = lax.dot_general(
            choose_ref[2 * t * PAIRS : 2 * (t + 1) * PAIRS], rows, NT, preferred_element_type=f32
        )
        picked[t], picked[t + 2] = both[:PAIRS], both[PAIRS:]
    low_half = lax.broadcasted_iota(jnp.int32, (PAIRS, 128), 1) < 64
    inputs = []
    for window in range(3):
        lanes = slice(128, 256) if window == 2 else slice(0, 128)
        groups = []
        for g in range(2):
            near, far = picked[2 * g][:, lanes], picked[2 * g + 1][:, lanes]
            if window == 1:
                groups.append(pltpu.roll(jnp.where(low_half, far, near), 64, 1))
            else:
                groups.append(jnp.where(low_half, near, far))
        inputs.append(jnp.concatenate(groups, axis=1).astype(bf16))
    inputs = jnp.concatenate(inputs, axis=0)

    lane = lax.broadcasted_iota(jnp.int32, (1, 256), 1)
    first_column = (lax.broadcasted_iota(jnp.int32, (1, 1, 256), 2) % 128) < 64

    def store(level, block, half_pre, x_out, m_out):
        blocks = 10 - level
        over = LAYERS - level
        value = half_pre * jnp.tanh(half_pre) + half_pre
        if 2 * block < over or 2 * block + 2 > 2 * blocks - over:
            row = strip * ROWS - over + 2 * block
            inside = [((row + r >= 0) & (row + r < strip_count * ROWS)).astype(f32) for r in range(2)]
            value = value * jnp.where(lane < 128, inside[0], inside[1])
        value = value.reshape(SLABS, LANE_ROWS, 256)
        edge = jnp.zeros((1, 1, 256), f32)
        after = jnp.concatenate([value[0:1, 1:], edge], axis=1)
        before = jnp.concatenate([edge, value[SLABS - 1 :, : LANE_ROWS - 1]], axis=1)
        right = jnp.concatenate([value[1:], after], axis=0)
        left = jnp.concatenate([before, value[: SLABS - 1]], axis=0)
        beside = jnp.where(first_column, right, left)
        x_out[block] = value.reshape(PAIRS, 256).astype(bf16)
        m_out[block] = beside.reshape(PAIRS, 256).astype(bf16)

    widen(mid_ref, wide_ref, 0)
    for step in range(3):
        half_pre = lax.dot_general(inputs, first_ref[step], NT, preferred_element_type=f32)
        for window in range(3):
            part = half_pre[window * PAIRS : (window + 1) * PAIRS]
            store(1, 3 * window + step, part + bias_ref[...], xa, ma)

    x_in, m_in, x_out, m_out = xa, ma, xb, mb
    for level in range(2, LAYERS):
        blocks = 10 - level
        if level < LAYERS - 1:
            widen(mid_ref, wide_ref, level - 1)
        for start in range(0, blocks, CHUNK):
            count = min(CHUNK, blocks - start)
            total = None
            for tile in range(4):
                source = m_in if tile // 2 else x_in
                at = start + tile % 2
                term = lax.dot_general(
                    source[at : at + count].reshape(count * PAIRS, 256),
                    wide_ref[level - 2, tile],
                    NT,
                    preferred_element_type=f32,
                )
                total = term if total is None else total + term
            for k in range(count):
                store(level, start + k, total[k * PAIRS : (k + 1) * PAIRS], x_out, m_out)
        x_in, m_in, x_out, m_out = x_out, m_out, x_in, m_in

    ends = [[], []]
    for block in range(4):
        total = None
        for tile in range(4):
            source = m_in if tile // 2 else x_in
            term = lax.dot_general(
                last_ref[tile], source[block + tile % 2], NT, preferred_element_type=f32
            )
            total = term if total is None else total + term
        high = total.astype(bf16)
        low = (total - high.astype(f32)).astype(bf16)
        for c in range(2):
            at = 32 * c
            ends[c] += [high[at : at + 32], low[at : at + 32]]
    both = None
    for c in range(2):
        at = SHIFTS.index(c) * PAIRS
        term = jnp.dot(jnp.concatenate(ends[c], axis=0), choose_ref[at : at + PAIRS], preferred_element_type=f32)
        both = term if both is None else both + term
    for block in range(4):
        at = 64 * block
        sums = both[at : at + 32] + both[at + 32 : at + 64]
        for r in range(2):
            for ch in range(4):
                at = ch * ROWS + 2 * block + r
                velocity_ref[at : at + 1, :] = sums[16 * r + ch : 16 * r + ch + 1]

    state = state_ref[...]
    fine = state + wide_row(table_ref[half + 3]) * velocity_ref[...]
    jump_ref[...] = fine - wide_row(table_ref[half]) * state


def on_device(
    prev_states, observation, bounds, coarse_factor, time_weight, weight_in, weight_mid, weight_out
):
    tm_count, strip_count = lax.axis_size("tm"), lax.axis_size("strip")
    half = tm_count // 2
    f32, bf16 = jnp.float32, jnp.bfloat16
    vmem = pl.BlockSpec(memory_space=pltpu.VMEM)
    hbm = pl.BlockSpec(memory_space=pltpu.HBM)
    shape = jax.ShapeDtypeStruct
    stay = lambda x: pltpu.with_memory_space_constraint(x, pltpu.HBM)
    state = prev_states.reshape(4 * ROWS, COLS)
    taps = jnp.transpose(weight_in, (0, 1, 3, 2)).reshape(72, HID)
    state, features = pl.pallas_call(
        pack_kernel,
        out_shape=[
            shape((4 * ROWS, COLS), f32),
            shape((64, COLS), bf16),
        ],
        in_specs=[hbm] * 2,
        out_specs=[vmem] * 2,
        scratch_shapes=[pltpu.SemaphoreType.DMA((2,))],
        compiler_params=pltpu.CompilerParams(vmem_limit_bytes=4 * 2**20),
        name="pack",
    )(*map(stay, (state, observation.reshape(4 * ROWS, COLS))))
    swap = [
        pair for i in range(1, strip_count - 1, 2) for pair in ((i, i + 1), (i + 1, i))
    ]
    outer = lax.ppermute(features, "strip", swap)
    inner = lax.all_gather(
        features, "strip", axis_index_groups=[[i, i + 1] for i in range(0, strip_count, 2)]
    )

    tables = pl.pallas_call(
        lambda *refs: prepare_kernel(tm_count, *refs),
        out_shape=[
            shape((3, 256, 256), bf16),
            shape((4, 64, 256), bf16),
            shape((1, 256), f32),
            shape((half + 4, 4 * ROWS, 128), f32),
            shape(weight_mid.shape, bf16),
            shape((4 * PAIRS, COLS), bf16),
        ],
        in_specs=[hbm] * 4 + [vmem] * 2,
        out_specs=[vmem] * 6,
        scratch_shapes=[
            pltpu.SMEM(bounds.shape, jnp.int32),
            pltpu.SMEM((4, tm_count), f32),
            pltpu.VMEM((1, HID), f32),
            pltpu.SemaphoreType.DMA((4,)),
        ],
        compiler_params=pltpu.CompilerParams(vmem_limit_bytes=32 * 2**20),
        cost_estimate=pl.CostEstimate(flops=10**7, bytes_accessed=4 * 10**6, transcendentals=0),
        name="prepare",
    )(*map(stay, (bounds, coarse_factor.T, time_weight[None], weight_mid, taps, weight_out)))
    hidden = lambda: pltpu.VMEM((10, PAIRS, 256), bf16)
    jump = pl.pallas_call(
        lambda *refs: sweep_kernel(half, strip_count, *refs),
        out_shape=shape((4 * ROWS, COLS), f32),
        in_specs=[vmem] * 10,
        out_specs=vmem,
        scratch_shapes=[
            pltpu.VMEM((8, 24, COLS), f32),
            pltpu.VMEM((192, COLS), f32),
            pltpu.VMEM((4 * ROWS, COLS), f32),
            hidden(), hidden(), hidden(), hidden(),
            pltpu.VMEM((LAYERS - 2, 4, 256, 256), bf16),
        ],
        compiler_params=pltpu.CompilerParams(vmem_limit_bytes=48 * 2**20),
        cost_estimate=pl.CostEstimate(flops=4 * 10**9, bytes_accessed=4 * 10**6, transcendentals=2 * 10**6),
        name="sweep",
    )(outer, inner, features, state, *tables)
    pair = lax.all_gather(
        jump, "tm", axis_index_groups=[[2 * p + 1, 2 * p] for p in range(half)]
    )
    sent, base = pl.pallas_call(
        lambda *refs: spread_kernel(half, *refs),
        out_shape=[shape((half, 4 * ROWS, COLS), bf16), shape((4 * ROWS, COLS), f32)],
        in_specs=[vmem] * 2,
        out_specs=[vmem] * 2,
        compiler_params=pltpu.CompilerParams(vmem_limit_bytes=4 * 2**20),
        name="spread",
    )(pair, tables[3])
    groups = [[(2 * p + half + 2) % tm_count + j for p in range(half)] for j in range(2)]
    received = lax.all_to_all(sent, "tm", 0, 0, axis_index_groups=groups)
    result = base + jnp.sum(received.astype(f32), axis=0)
    return result.reshape(1, 4, ROWS, COLS)


def solution(mesh):
    placed = (P("tm", None, "strip", None), P(None, "strip", None), P(), P(), P(), P(), P(), P())
    return jax.shard_map(
        on_device,
        mesh=mesh,
        in_specs=placed,
        out_specs=P("tm", None, "strip", None),
        check_vma=False,
    )
```
